32 devices in a mesh: vol: 8 (over z, y), rep: 4 (over x, core).
Axes of the slice: x: 2, y: 2, z: 4, core: 2. Of those that a mesh axis runs over, the one named last changes fastest.
Arguments:
- surface_state: float32 [896, 32, 128], P('vol', 'rep'), may hold values from -6 to 6
- direction: float32 [896, 32, 128], P('vol', 'rep'), may hold values from -6 to 6
- stiffness: float32 [896, 128], P('vol'), may hold values from 0.5 to 5
- partners: int32 [896, 4], P('vol'), may hold values from 0 to 895, as said below
- contact_owner: int32 [896], P('vol'), may hold values from 0 to 7, as said below
- projection: float32 [32, 32], replicated, may hold values from -1 to 1
- mortar: float32 [4, 128, 128], replicated, may hold values from -0.5 to 0.5
Outputs:
- hessian_product: float32 [896, 32, 128], P('vol', 'rep')
The draws below stay inside these ranges and needn't reach their ends.
Inputs may be any that keep to these rules, and one draw needn't show every extreme that they name: `contact_owner`: in the 112 blocks of one volume owner (aligned blocks of rows) no contact owner is named more than 28 times; 1 contact owners are named exactly 28 times in every such block. `partners`: partners may repeat, may be the block itself, and may have another contact owner than their block.
All inputs are finite; a program needn't handle non-finite values.
Results may differ from the reference program's by a relative error of at most 0.0001.
Values sent between devices are 32-bit elements; how exact they have to be, the bound alone decides.
No kernel may reach another device: no remote copies, remote signals or barrier semaphores. Data moves between devices by JAX's collectives and lax.ppermute only.
A program may use at most 64 MiB of HBM per device.

```python
import math
import jax
import jax.numpy as jnp
from jax import lax

FACES = 128
CHANNELS = 32
PARTNERS = 4
BLK_DEV = 112
NB = 896
CAP = 28
HOT = 1
N_VOL = 8


def route_table(key):
    folded = jax.random.fold_in(key, 7)
    key_hot, key_len, key_score, key_block = jax.random.split(folded, 4)
    half_cap = (CAP + 1) // 2
    hot_order = jax.random.permutation(key_hot, N_VOL).astype(jnp.int32)
    hot_rank = jnp.argsort(hot_order).astype(jnp.int32)
    is_cold = (hot_rank >= HOT).astype(jnp.int32)
    dest_iota = jnp.arange(N_VOL, dtype=jnp.int32)
    scores = jax.random.randint(key_score, (N_VOL, N_VOL), 0, 1024)
    sort_keys = (is_cold[None, :] * 1024 + scores) * N_VOL + dest_iota[None, :]
    dest_order = jnp.argsort(sort_keys, axis=1).astype(jnp.int32)
    lengths = jax.random.randint(key_len, (N_VOL, N_VOL), half_cap, CAP + 1)
    lengths = jnp.where(dest_iota[None, :] < HOT, CAP, lengths)
    run_ends = jnp.cumsum(lengths, axis=1)
    positions = jnp.arange(BLK_DEV, dtype=jnp.int32)
    groups = jnp.sum((run_ends[:, None, :] <= positions[None, :, None]).astype(jnp.int32), axis=2)
    targets = jnp.take_along_axis(dest_order, groups, axis=1)
    block_scores = jax.random.randint(key_block, (N_VOL, BLK_DEV), 0, 1024) * BLK_DEV + positions[None, :]
    shuffled = jnp.argsort(block_scores, axis=1).astype(jnp.int32)
    inverse = jnp.argsort(shuffled, axis=1).astype(jnp.int32)
    owners = jnp.take_along_axis(targets, inverse, axis=1)
    return owners.reshape(NB).astype(jnp.int32)


def draw_contact_owner(key, part):
    return route_table(key)


def draw_partners(key, part):
    owners = route_table(key)
    sorted_blocks = jnp.argsort(owners, stable=True).astype(jnp.int32)
    counts = jax.ops.segment_sum(jnp.ones(NB, jnp.int32), owners, num_segments=N_VOL)
    starts = jnp.cumsum(counts) - counts
    drawn_picks = jax.random.randint(jax.random.fold_in(key, 11), (NB, PARTNERS), 0, 1 << 20)
    drawn_picks = drawn_picks % counts[owners][:, None]
    local_picks = sorted_blocks[starts[owners][:, None] + drawn_picks].astype(jnp.int32)
    cross_picks = jax.random.randint(jax.random.fold_in(key, 13), (NB, PARTNERS), 0, NB).astype(jnp.int32)
    flags = jax.random.randint(jax.random.fold_in(key, 17), (NB, PARTNERS), 0, 8)
    return jnp.where(flags == 0, cross_picks, local_picks).astype(jnp.int32)


def levels(own_key, shape, shards, smallest, largest):
    factor_of, own = 1.0, jax.random.fold_in(own_key, 6)
    for position, blocks in shards:
        heights = jnp.exp(jax.random.uniform(jax.random.fold_in(own, position), (blocks,), jnp.float32, smallest / len(shards), largest / len(shards)))
        factor_of = factor_of * jnp.repeat(heights, shape[position] // blocks).reshape([-1 if axis == position else 1 for axis in range(len(shape))])
    return factor_of


def normal_values(own_key, shape, spread, limit, cuts=(), kind=jnp.bfloat16):
    drawn = spread * jax.random.normal(own_key, shape, jnp.float32)
    if cuts:
        drawn = drawn * levels(own_key, shape, cuts, -0.22, 0.18)
    return jnp.clip(drawn, -limit, limit).astype(kind)


def setup_inputs(seed: int = 0) -> dict:
    seeds = jax.random.split(jax.random.key(seed), 8)
    surface_state = normal_values(seeds[0], (NB, CHANNELS, FACES), 1.0, 6.0, ((0, 8), (1, 4)), jnp.float32)
    direction = normal_values(seeds[1], (NB, CHANNELS, FACES), 1.0, 6.0, ((0, 8), (1, 4)), jnp.float32)
    stiffness = jnp.clip(jnp.exp(math.log(5.0) - 2.3025851 * jax.random.uniform(seeds[2], (NB, FACES), jnp.float32) ** levels(seeds[2], (NB, FACES), ((0, 8),), -0.2, 0.2)), 0.5, 5.0)
    partners = draw_partners(jax.random.fold_in(seeds[7], 71), 0)
    contact_owner = draw_contact_owner(jax.random.fold_in(seeds[7], 71), 0)
    projection = normal_values(seeds[5], (CHANNELS, CHANNELS), CHANNELS ** -0.5, 1.0, (), jnp.float32)
    mortar = normal_values(seeds[6], (PARTNERS, FACES, FACES), FACES ** -0.5, 0.5, (), jnp.float32)
    return dict(surface_state=surface_state, direction=direction, stiffness=stiffness, partners=partners, contact_owner=contact_owner, projection=projection, mortar=mortar)


sharpness = 1.5


def reference(surface_state, direction, stiffness, partners, contact_owner, projection, mortar):
    highest = lax.Precision.HIGHEST
    projected = jnp.einsum("ij,bjf->bif", projection, surface_state, precision=highest)
    moving = jnp.einsum("ij,bjf->bif", projection, direction, precision=highest)
    block_total = surface_state.shape[0]
    tangent = jnp.zeros_like(projected)
    returned = jnp.zeros_like(projected)
    for column in range(PARTNERS):
        target = partners[:, column].astype(jnp.int32)
        mapped_state = jnp.einsum("bcf,fg->bcg", projected[target], mortar[column], precision=highest)
        mapped_move = jnp.einsum("bcf,fg->bcg", moving[target], mortar[column], precision=highest)
        contact_gap = projected - mapped_state
        squashed = jax.nn.sigmoid(sharpness * contact_gap)
        agree = (contact_owner == contact_owner[target]).astype(jnp.float32)
        weight = agree[:, None, None] * stiffness[:, None, :] * sharpness * squashed * (1.0 - squashed)
        traction = weight * (moving - mapped_move)
        tangent = tangent + traction
        gathered_back = jax.ops.segment_sum(traction, target, num_segments=block_total)
        returned = returned + jnp.einsum("bcg,fg->bcf", gathered_back, mortar[column], precision=highest)
    summed = tangent - returned
    return jnp.einsum("ji,bjf->bif", projection, summed, precision=highest)
```

```python
import functools

import jax
import jax.numpy as jnp
from jax import lax
from jax.experimental import pallas as pl
from jax.experimental.pallas import tpu as pltpu
from jax.sharding import PartitionSpec as P

sharpness = 1.5
LANES = 128
ROWS = 8


def halves(value):
    high = value.astype(jnp.bfloat16)
    low = (value - high.astype(jnp.float32)).astype(jnp.bfloat16)
    return high, low


def product(a, b):
    return jnp.dot(a, b, preferred_element_type=jnp.float32)


def product3(a, b):
    return product(a[0], b[0]) + product(a[1], b[0]) + product(a[0], b[1])


def iota(shape, dim):
    return lax.broadcasted_iota(jnp.int32, shape, dim)


def one_where(cond):
    return jnp.where(cond, 1.0, 0.0).astype(jnp.bfloat16)


def mixer(projection, rep_index, rep_count, share, group, pack):
    channels = projection.shape[0]
    inner = group // pack
    size = channels * group
    row = iota((size, channels), 0)
    spread = one_where(row // group == iota((size, channels), 1))
    col = iota((channels, size), 1)
    d = col // (group * share)
    j = (rep_index ^ d) * share + col % share
    pick = one_where(iota((channels, size), 0) == j)
    r = iota((size, size), 0)
    c = iota((size, size), 1)
    row_slot = r % group
    col_slot = ((c // share) % inner) * pack + (c // (share * inner)) % pack
    keep = row_slot == col_slot
    out = []
    for part in halves(projection):
        wide = product(product(spread, part).astype(jnp.bfloat16), pick)
        out.append(jnp.where(keep, wide, 0.0).astype(jnp.bfloat16))
    return out


def project_kernel(rep_count, share, place_ref, projection_ref, *refs):
    out_ref = refs[-1]
    state_refs, move_refs = refs[:rep_count], refs[rep_count : 2 * rep_count]
    channels, rows, faces = out_ref.shape
    group = ROWS
    per = group // 2 * share
    mix = mixer(projection_ref[...], place_ref[0], rep_count, share, group, 2)
    for g in range(rows // group):
        span = pl.ds(g * per, per)
        pieces = []
        for d in range(rep_count):
            pieces += [state_refs[d][span, :], move_refs[d][span, :]]
        values = halves(jnp.concatenate(pieces, axis=0))
        out = product3(mix, values)
        out_ref[:, pl.ds(g * group, group), :] = out.reshape(channels, group, faces)


def back_kernel(rep_count, share, place_ref, projection_ref, summed_ref, out_ref):
    channels, padded, faces = summed_ref.shape
    group = ROWS
    size = channels * group
    mix = mixer(projection_ref[...], place_ref[0], rep_count, share, group, 1)
    mix = [m.T for m in mix]
    rows = out_ref.shape[1]
    for g in range(padded // group):
        values = halves(summed_ref[:, pl.ds(g * group, group), :].reshape(size, faces))
        out = product3(mix, values).reshape(rep_count, group * share, faces)
        count = min(group * share, rows - g * group * share)
        out_ref[:, pl.ds(g * group * share, count), :] = out[:, :count]


def contact_kernel(
    order, blocks, partner_count, place_ref, packed_ref, notes_ref, mortar_ref, out_ref,
    stiff_ref, columns_ref, rows_ref, mapped_ref, hot_ref, back_ref, acc_ref, tangent_ref,
):
    total, faces = stiff_ref.shape
    me = place_ref[0]
    for at, d in enumerate(order):
        start = pl.multiple_of((me ^ d) * blocks, ROWS)
        stiff_ref[pl.ds(start, blocks), :] = notes_ref[at, 0:blocks, :]
        small = notes_ref[at, blocks : blocks + ROWS, :]
        square = jnp.concatenate([small, jnp.zeros((LANES - ROWS, LANES), jnp.float32)], axis=0)
        columns_ref[pl.ds(start, blocks), :] = square.T[:blocks]
    for t in range(total // LANES):
        rows_ref[:, t * LANES : (t + 1) * LANES] = columns_ref[t * LANES : (t + 1) * LANES, :].T[:ROWS]

    state = packed_ref[pl.ds(0, total, stride=2), :]
    move = packed_ref[pl.ds(1, total, stride=2), :]
    state_parts, move_parts = halves(state), halves(move)
    tangent_ref[...] = jnp.zeros_like(tangent_ref)
    acc_ref[...] = jnp.zeros_like(acc_ref)
    owner_row = rows_ref[partner_count : partner_count + 1, :]
    owner_column = columns_ref[:, partner_count : partner_count + 1]

    for k in range(partner_count):
        mortar = halves(mortar_ref[k])
        for part, parts in enumerate((state_parts, move_parts)):
            high, low = halves(product3(parts, mortar))
            mapped_ref[0, :, part * faces : (part + 1) * faces] = high
            mapped_ref[1, :, part * faces : (part + 1) * faces] = low
        target = columns_ref[:, k : k + 1]
        named = iota((total, total), 1).astype(jnp.float32) == target
        hot_ref[...] = one_where(named)
        partner_owner = jnp.sum(jnp.where(named, owner_row, 0.0), axis=1, keepdims=True)
        agree = (partner_owner == owner_column).astype(jnp.float32)
        gathered = product(hot_ref[...], mapped_ref[0]) + product(hot_ref[...], mapped_ref[1])
        gap = packed_ref[pl.ds(0, total, stride=2), :] - gathered[:, :faces]
        change = packed_ref[pl.ds(1, total, stride=2), :] - gathered[:, faces:]
        small = jnp.exp(-sharpness * jnp.abs(gap))
        slope = small / ((1.0 + small) * (1.0 + small))
        traction = stiff_ref[...] * (agree * sharpness) * slope * change
        tangent_ref[...] += traction
        back = product3(halves(traction), halves(mortar_ref[k].T))
        high, low = halves(back)
        back_ref[:, :faces] = high
        back_ref[:, faces:] = low
        hot_ref[...] = one_where(iota((total, total), 0).astype(jnp.float32) == rows_ref[k : k + 1, :])
        acc_ref[...] += product(hot_ref[...], back_ref[...])

    tangent_ref[...] = tangent_ref[...] - acc_ref[:, :faces] - acc_ref[:, faces:]
    devices, padded, _ = out_ref.shape
    slab = total // devices
    for device in range(devices):
        out_ref[device, 0:slab, :] = tangent_ref[device * slab : (device + 1) * slab, :]
        if padded > slab:
            out_ref[device, slab:padded, :] = jnp.zeros((padded - slab, faces), jnp.float32)


def spread_local(surface_state, direction, stiffness, partners, contact_owner, projection, mortar):
    vol_count, rep_count = lax.axis_size("vol"), lax.axis_size("rep")
    devices = vol_count * rep_count
    vol_index, rep_index = lax.axis_index("vol"), lax.axis_index("rep")
    blocks, share, faces = surface_state.shape
    channels = projection.shape[0]
    partner_count = partners.shape[1]
    slab = blocks // rep_count
    padded = -(-slab // ROWS) * ROWS
    total = blocks * vol_count
    vmem = pl.BlockSpec(memory_space=pltpu.VMEM)
    smem = pl.BlockSpec(memory_space=pltpu.SMEM)
    rep_place = rep_index.astype(jnp.int32)[None]
    vol_place = vol_index.astype(jnp.int32)[None]
    params = pltpu.CompilerParams(vmem_limit_bytes=48 * 1024 * 1024)

    small = jnp.concatenate([partners.T, contact_owner[None, :]], axis=0).astype(jnp.float32)
    small = jnp.pad(small, ((0, ROWS - partner_count - 1), (0, faces - blocks)))
    notes = jnp.concatenate([stiffness, small], axis=0)[None]
    order = [0]
    step = vol_count // 2
    while step:
        other = lax.ppermute(notes, "vol", [(i, i ^ step) for i in range(vol_count)])
        notes = jnp.concatenate([notes, other], axis=0)
        order += [d ^ step for d in order]
        step //= 2

    def slabs(values):
        return [
            lax.dynamic_slice_in_dim(values, (rep_index ^ d) * slab, slab, 0).reshape(slab * share, faces)
            for d in range(rep_count)
        ]

    def exchange(pieces):
        return pieces[:1] + [
            lax.ppermute(pieces[d], "rep", [(i, i ^ d) for i in range(rep_count)])
            for d in range(1, rep_count)
        ]

    both = [jnp.stack(pair) for pair in zip(slabs(surface_state), slabs(direction))]
    both = exchange(both)
    sent = pl.pallas_call(
        functools.partial(project_kernel, rep_count, share),
        out_shape=jax.ShapeDtypeStruct((channels, 2 * slab, faces), jnp.float32),
        in_specs=[smem] + [vmem] * (1 + 2 * rep_count),
        out_specs=vmem,
        compiler_params=params,
    )(rep_place, projection, *[b[0] for b in both], *[b[1] for b in both])
    packed = lax.all_to_all(sent, ("vol", "rep"), 0, 0, tiled=True).reshape(2 * total, faces)

    summed = pl.pallas_call(
        functools.partial(contact_kernel, tuple(order), blocks, partner_count),
        out_shape=jax.ShapeDtypeStruct((devices, padded, faces), jnp.float32),
        in_specs=[smem, vmem, vmem, vmem],
        out_specs=vmem,
        scratch_shapes=[
            pltpu.VMEM((total, faces), jnp.float32),
            pltpu.VMEM((total, LANES), jnp.float32),
            pltpu.VMEM((ROWS, total), jnp.float32),
            pltpu.VMEM((2, total, 2 * faces), jnp.bfloat16),
            pltpu.VMEM((total, total), jnp.bfloat16),
            pltpu.VMEM((total, 2 * faces), jnp.bfloat16),
            pltpu.VMEM((total, 2 * faces), jnp.float32),
            pltpu.VMEM((total, faces), jnp.float32),
        ],
        compiler_params=params,
    )(vol_place, packed, notes, mortar)
    returned = lax.all_to_all(summed, ("vol", "rep"), 0, 0, tiled=True)

    pieces = pl.pallas_call(
        functools.partial(back_kernel, rep_count, share),
        out_shape=jax.ShapeDtypeStruct((rep_count, slab * share, faces), jnp.float32),
        in_specs=[smem, vmem, vmem],
        out_specs=vmem,
        compiler_params=params,
    )(rep_place, projection, returned)
    pieces = exchange([pieces[d] for d in range(rep_count)])
    out = jnp.zeros((blocks * share, faces), jnp.float32)
    for d in range(rep_count):
        out = lax.dynamic_update_slice_in_dim(out, pieces[d], (rep_index ^ d) * slab * share, 0)
    return out.reshape(blocks, share, faces)


def routed_local(surface_state, direction, stiffness, partners, contact_owner, projection, mortar):
    highest = lax.Precision.HIGHEST
    vol_count = lax.axis_size("vol")
    rep_index = lax.axis_index("rep")
    vol_index = lax.axis_index("vol")
    blocks, channel_share, face_count = surface_state.shape
    partner_count = partners.shape[1]
    capacity = max(2, (2 * blocks + vol_count - 1) // vol_count)
    slot_count = vol_count * capacity
    my_columns = lax.dynamic_slice_in_dim(projection, rep_index * channel_share, channel_share, 1)
    my_rows = lax.dynamic_slice_in_dim(projection, rep_index * channel_share, channel_share, 0)

    def fold_one(piece):
        return jnp.einsum("ij,bjf->bif", my_rows, piece, precision=highest)

    counter = jnp.arange(blocks, dtype=jnp.int32)
    same_owner = contact_owner[:, None] == contact_owner[None, :]
    earlier = counter[:, None] < counter[None, :]
    bucket_rank = jnp.sum((same_owner & earlier).astype(jnp.int32), axis=0)
    slot_of = contact_owner * capacity + bucket_rank
    slot_iota = jnp.arange(slot_count, dtype=jnp.int32)
    matches = slot_iota[:, None] == slot_of[None, :]
    occupied = jnp.any(matches, axis=1).astype(jnp.float32)
    source_row = jnp.sum(jnp.where(matches, counter[None, :], 0), axis=1)
    global_ids = vol_index * blocks + counter
    labels = jnp.concatenate([(global_ids + 1)[:, None], partners], axis=1).astype(jnp.float32)
    send_stiff = (stiffness[source_row] * occupied[:, None]).reshape(
        vol_count, capacity, face_count
    )
    send_labels = (labels[source_row] * occupied[:, None]).reshape(
        vol_count, capacity, partner_count + 1
    )

    def pack(values):
        return (values[source_row] * occupied[:, None, None]).reshape(
            vol_count, capacity, channel_share, face_count
        )

    projected = fold_one(lax.all_gather(surface_state, "rep", axis=1, tiled=True))
    moving = fold_one(lax.all_gather(direction, "rep", axis=1, tiled=True))
    received = (
        lax.all_to_all(pack(projected), "vol", split_axis=0, concat_axis=0, tiled=True),
        lax.all_to_all(pack(moving), "vol", split_axis=0, concat_axis=0, tiled=True),
        lax.all_to_all(send_stiff, "vol", split_axis=0, concat_axis=0, tiled=True),
        lax.all_to_all(send_labels, "vol", split_axis=0, concat_axis=0, tiled=True),
    )
    got_state = received[0].reshape(slot_count, channel_share, face_count)
    got_move = received[1].reshape(slot_count, channel_share, face_count)
    got_stiff = received[2].reshape(slot_count, face_count)
    got_labels = received[3].reshape(slot_count, partner_count + 1).astype(jnp.int32)
    slot_ids = got_labels[:, 0] - 1
    partner_ids = got_labels[:, 1:]
    partner_source = partner_ids // blocks
    candidates = slot_ids.reshape(vol_count, capacity)[partner_source]
    offsets = jnp.arange(capacity, dtype=jnp.int32)
    matched = candidates == partner_ids[..., None]
    found = jnp.any(matched, axis=2).astype(jnp.float32)
    partner_offset = jnp.sum(jnp.where(matched, offsets, 0), axis=2)
    partner_slot = partner_source * capacity + partner_offset
    mapped_state = jnp.einsum("rcf,kfg->krcg", got_state, mortar, precision=highest)
    weights = []
    for column in range(partner_count):
        target = partner_slot[:, column]
        contact_gap = got_state - mapped_state[column][target]
        squashed = jax.nn.sigmoid(sharpness * contact_gap)
        weights.append(
            found[:, column][:, None, None]
            * got_stiff[:, None, :]
            * sharpness
            * squashed
            * (1.0 - squashed)
        )
    partner_slot, weights = (partner_slot, weights)
    mapped_move = jnp.einsum("rcf,kfg->krcg", got_move, mortar, precision=highest)
    tangent = jnp.zeros_like(got_move)
    returns = []
    for column in range(partner_count):
        target = partner_slot[:, column]
        traction = weights[column] * (got_move - mapped_move[column][target])
        tangent = tangent + traction
        returns.append(jax.ops.segment_sum(traction, target, num_segments=slot_count))
    returned = jnp.einsum("krcg,kfg->rcf", jnp.stack(returns), mortar, precision=highest)
    summed = (tangent - returned).reshape(vol_count, capacity, channel_share, face_count)
    returned_tiles = lax.all_to_all(summed, "vol", split_axis=0, concat_axis=0, tiled=True)
    own_tangent = returned_tiles.reshape(slot_count, channel_share, face_count)[slot_of]
    return jnp.einsum(
        "ji,bjf->bif",
        my_columns,
        lax.all_gather(own_tangent, "rep", axis=1, tiled=True),
        precision=highest,
    )


def one_channel_each(mesh, state_shape, partner_shape):
    vol_count, rep_count = mesh.shape["vol"], mesh.shape["rep"]
    total, channels, faces = state_shape
    blocks = total // vol_count
    powers = all(n & (n - 1) == 0 for n in (vol_count, rep_count))
    return (
        powers
        and channels == vol_count * rep_count
        and channels // rep_count == ROWS
        and faces == LANES
        and blocks <= faces
        and blocks % (ROWS // 2 * rep_count) == 0
        and total % LANES == 0
        and partner_shape[1] < ROWS
    )


def solution(mesh):
    placed = (
        P("vol", "rep", None),
        P("vol", "rep", None),
        P("vol", None),
        P("vol", None),
        P("vol"),
        P(),
        P(),
    )

    def program(surface_state, direction, stiffness, partners, *rest):
        fits = one_channel_each(mesh, surface_state.shape, partners.shape)
        plan = spread_local if fits else routed_local
        return jax.shard_map(
            plan, mesh=mesh, in_specs=placed, out_specs=P("vol", "rep", None), check_vma=False
        )(surface_state, direction, stiffness, partners, *rest)

    return program
```

```python
import functools

import jax
import jax.numpy as jnp
from jax import lax
from jax.experimental import pallas as pl
from jax.experimental.pallas import tpu as pltpu
from jax.sharding import PartitionSpec as P

sharpness = 1.5
LANES = 128
ROWS = 8


def halves(value):
    high = value.astype(jnp.bfloat16)
    low = (value - high.astype(jnp.float32)).astype(jnp.bfloat16)
    return high, low


def product(a, b):
    return jnp.dot(a, b, preferred_element_type=jnp.float32)


def product3(a, b):
    return product(a[0], b[0]) + product(a[1], b[0]) + product(a[0], b[1])


def three_parts(value):
    high, low = halves(value)
    return high, high, low


def iota(shape, dim):
    return lax.broadcasted_iota(jnp.int32, shape, dim)


def one_where(cond):
    return jnp.where(cond, 1.0, 0.0).astype(jnp.bfloat16)


def mixer(projection, rep_index, rep_count, share, group, pack):
    channels = projection.shape[0]
    inner = group // pack
    size = channels * group
    row = iota((size, channels), 0)
    spread = one_where(row // group == iota((size, channels), 1))
    col = iota((channels, size), 1)
    d = col // (group * share)
    j = (rep_index ^ d) * share + col % share
    pick = one_where(iota((channels, size), 0) == j)
    r = iota((size, size), 0)
    c = iota((size, size), 1)
    row_slot = r % group
    col_slot = ((c // share) % inner) * pack + (c // (share * inner)) % pack
    keep = row_slot == col_slot
    out = []
    for part in halves(projection):
        wide = product(product(spread, part).astype(jnp.bfloat16), pick)
        out.append(jnp.where(keep, wide, 0.0).astype(jnp.bfloat16))
    return out


def mixers_kernel(rep_count, share, place_ref, projection_ref, mix_ref, back_mix_ref):
    projection = projection_ref[...]
    for part, value in enumerate(mixer(projection, place_ref[0], rep_count, share, ROWS, 2)):
        mix_ref[part] = value
    for part, value in enumerate(mixer(projection, place_ref[0], rep_count, share, ROWS, 1)):
        back_mix_ref[part] = value.astype(jnp.float32).T.astype(jnp.bfloat16)


def project_kernel(rep_count, share, mix_ref, *refs):
    out_ref = refs[-1]
    state_refs, move_refs = refs[:rep_count], refs[rep_count : 2 * rep_count]
    channels, rows, faces = out_ref.shape
    group = ROWS
    per = group // 2 * share
    mix = mix_ref[0], mix_ref[1]
    for g in range(rows // group):
        span = pl.ds(g * per, per)
        pieces = []
        for d in range(rep_count):
            pieces += [state_refs[d][span, :], move_refs[d][span, :]]
        values = halves(jnp.concatenate(pieces, axis=0))
        out = product3(mix, values)
        out_ref[:, pl.ds(g * group, group), :] = out.reshape(channels, group, faces)


def back_kernel(rep_count, share, mix_ref, summed_ref, out_ref):
    channels, padded, faces = summed_ref.shape
    group = ROWS
    size = channels * group
    mix = mix_ref[0], mix_ref[1]
    rows = out_ref.shape[1]
    for g in range(padded // group):
        values = halves(summed_ref[:, pl.ds(g * group, group), :].reshape(size, faces))
        out = product3(mix, values).reshape(rep_count, group * share, faces)
        count = min(group * share, rows - g * group * share)
        out_ref[:, pl.ds(g * group * share, count), :] = out[:, :count]


def route_kernel(
    order, partner_count, places_ref, notes_ref, mortar_ref, columns_ref, weight_ref, mortar_parts_ref, turned_parts_ref,
    stiff_ref,
):
    total, faces = stiff_ref.shape
    vol_count = len(order)
    blocks = total // vol_count
    half = blocks // 2
    me, mine = places_ref[0], places_ref[1]
    for at, d in enumerate(order):
        start = pl.multiple_of((me ^ d) * blocks, ROWS)
        for side in range(2):
            first = pl.multiple_of(start + (mine ^ side) * half, ROWS)
            stiff_ref[pl.ds(first, half), :] = notes_ref[side, at, 0:half, :]
        small = notes_ref[0, at, half : half + ROWS, :]
        square = jnp.concatenate([small, jnp.zeros((LANES - ROWS, LANES), jnp.float32)], axis=0)
        columns_ref[pl.ds(start, blocks), :] = square.T[:blocks]
    owner_column = columns_ref[:, partner_count : partner_count + 1]
    owners = jnp.broadcast_to(owner_column, (total, faces))
    small_owners = owners.astype(jnp.bfloat16)
    for k in range(partner_count):
        hot = one_where(iota((total, total), 1).astype(jnp.float32) == columns_ref[:, k : k + 1])
        agree = product(hot, small_owners) == owners
        weight_ref[k] = jnp.where(agree, stiff_ref[...] * sharpness, 0.0)
    for k in range(partner_count):
        for at, part in enumerate(three_parts(mortar_ref[k])):
            mortar_parts_ref[at * faces : (at + 1) * faces, k * faces : (k + 1) * faces] = part
        for at, part in enumerate(three_parts(mortar_ref[k].T)):
            turned_parts_ref[k, at * faces : (at + 1) * faces, :] = part


def contact_kernel(
    packed_ref, columns_ref, weight_ref, mortar_parts_ref, turned_parts_ref, out_ref,
    mapped_ref, back_ref, tangent_ref, rows_ref,
):
    partner_count, total, faces = weight_ref.shape
    rows = total // 2
    tiles = [(k, r) for k in range(partner_count) for r in range(0, total, rows)]
    for t in range(total // LANES):
        rows_ref[:, t * LANES : (t + 1) * LANES] = columns_ref[t * LANES : (t + 1) * LANES, :].T[:ROWS]
    for which in range(2):
        high, low = halves(packed_ref[pl.ds(which, total, stride=2), :])
        mapped = product(jnp.concatenate([high, low, high], axis=1), mortar_parts_ref[...])
        for k in range(partner_count):
            high, low = halves(mapped[:, k * faces : (k + 1) * faces])
            mapped_ref[k, 0, :, which * faces : (which + 1) * faces] = high
            mapped_ref[k, 1, :, which * faces : (which + 1) * faces] = low

    def gather(k, r):
        named = iota((rows, total), 1).astype(jnp.float32) == columns_ref[pl.ds(r, rows), k : k + 1]
        hot = one_where(named)
        return product(hot, mapped_ref[k, 0]) + product(hot, mapped_ref[k, 1])

    def traction_parts(k, r, gathered):
        gap = packed_ref[pl.ds(2 * r, rows, stride=2), :] - gathered[:, :faces]
        change = packed_ref[pl.ds(2 * r + 1, rows, stride=2), :] - gathered[:, faces:]
        small = jnp.exp(-sharpness * jnp.abs(gap))
        slope = small / ((1.0 + small) * (1.0 + small))
        traction = weight_ref[k, pl.ds(r, rows), :] * slope * change
        if k == 0:
            tangent_ref[pl.ds(r, rows), :] = traction
        else:
            tangent_ref[pl.ds(r, rows), :] += traction
        high, low = halves(traction)
        return jnp.concatenate([high, low, high], axis=1)

    def send_back(k, r, parts):
        high, low = halves(product(parts, turned_parts_ref[k]))
        back_ref[k, pl.ds(r, rows), :faces] = high
        back_ref[k, pl.ds(r, rows), faces:] = low

    ahead = 2
    gathered = {at: gather(*tiles[at]) for at in range(ahead)}
    waiting = None
    for at, (k, r) in enumerate(tiles):
        if at + ahead < len(tiles):
            gathered[at + ahead] = gather(*tiles[at + ahead])
        parts = traction_parts(k, r, gathered.pop(at))
        if waiting is not None:
            send_back(*waiting)
        waiting = k, r, parts
    send_back(*waiting)

    def turned(k, r):
        return one_where((iota((rows, total), 0) + r).astype(jnp.float32) == rows_ref[k : k + 1, :])

    for r in range(0, total, rows):
        span = pl.ds(r, rows)
        back = product(turned(0, r), back_ref[0])
        for k in range(1, partner_count):
            back += product(turned(k, r), back_ref[k])
        tangent_ref[span, :] = tangent_ref[span, :] - back[:, :faces] - back[:, faces:]
    devices, padded, _ = out_ref.shape
    slab = total // devices
    for device in range(devices):
        out_ref[device, 0:slab, :] = tangent_ref[device * slab : (device + 1) * slab, :]
        if padded > slab:
            out_ref[device, slab:padded, :] = jnp.zeros((padded - slab, faces), jnp.float32)


def spread_local(surface_state, direction, stiffness, partners, contact_owner, projection, mortar):
    vol_count, rep_count = lax.axis_size("vol"), lax.axis_size("rep")
    devices = vol_count * rep_count
    vol_index, rep_index = lax.axis_index("vol"), lax.axis_index("rep")
    blocks, share, faces = surface_state.shape
    channels = projection.shape[0]
    partner_count = partners.shape[1]
    slab = blocks // rep_count
    padded = -(-slab // ROWS) * ROWS
    total = blocks * vol_count
    size = channels * ROWS
    vmem = pl.BlockSpec(memory_space=pltpu.VMEM)
    smem = pl.BlockSpec(memory_space=pltpu.SMEM)
    rep_place = rep_index.astype(jnp.int32)[None]
    params = pltpu.CompilerParams(vmem_limit_bytes=18 * 1024 * 1024)

    def array(*shape, dtype=jnp.float32):
        return jax.ShapeDtypeStruct(shape, dtype)

    def swap(value, axis, d):
        count = lax.axis_size(axis)
        return lax.ppermute(value, axis, [(i, i ^ d) for i in range(count)])

    def slabs(values):
        return [
            lax.dynamic_slice_in_dim(values, (rep_index ^ d) * slab, slab, 0).reshape(slab * share, faces)
            for d in range(rep_count)
        ]

    def exchange(pieces):
        return pieces[:1] + [swap(pieces[d], "rep", d) for d in range(1, rep_count)]

    both = exchange([jnp.stack(pair) for pair in zip(slabs(surface_state), slabs(direction))])

    half = blocks // 2
    small = jnp.concatenate([partners.T, contact_owner[None, :]], axis=0).astype(jnp.float32)
    small = jnp.pad(small, ((0, ROWS - partner_count - 1), (0, faces - blocks)))
    mine = rep_index % 2
    notes = jnp.concatenate([lax.dynamic_slice_in_dim(stiffness, mine * half, half, 0), small], axis=0)
    far = list(range(2, vol_count, 2))
    notes = jnp.stack([notes] + [swap(notes, "vol", d) for d in far])
    notes = jnp.concatenate([notes, swap(notes, "vol", 1)], axis=0)
    order = [0] + far + [1] + [d ^ 1 for d in far]

    mix, back_mix = pl.pallas_call(
        functools.partial(mixers_kernel, rep_count, share),
        out_shape=(array(2, size, size, dtype=jnp.bfloat16), array(2, size, size, dtype=jnp.bfloat16)),
        in_specs=[smem, vmem],
        out_specs=(vmem,) * 2,
        compiler_params=params,
    )(rep_place, projection)

    both, notes = lax.optimization_barrier((both, notes))
    sent = pl.pallas_call(
        functools.partial(project_kernel, rep_count, share),
        out_shape=array(channels, 2 * slab, faces),
        in_specs=[vmem] * (1 + 2 * rep_count),
        out_specs=vmem,
        compiler_params=params,
    )(mix, *[b[0] for b in both], *[b[1] for b in both])
    packed = lax.all_to_all(sent, ("vol", "rep"), 0, 0, tiled=True).reshape(2 * total, faces)

    notes = jnp.stack([notes, swap(notes, "rep", 1)])
    columns, weight, mortar_parts, turned_parts = pl.pallas_call(
        functools.partial(route_kernel, tuple(order), partner_count),
        out_shape=(
            array(total, LANES),
            array(partner_count, total, faces),
            array(3 * faces, partner_count * faces, dtype=jnp.bfloat16),
            array(partner_count, 3 * faces, faces, dtype=jnp.bfloat16),
        ),
        in_specs=[smem, vmem, vmem],
        out_specs=(vmem,) * 4,
        scratch_shapes=[pltpu.VMEM((total, faces), jnp.float32)],
        compiler_params=params,
    )(jnp.stack([vol_index, mine]).astype(jnp.int32), notes, mortar)

    summed = pl.pallas_call(
        contact_kernel,
        out_shape=array(devices, padded, faces),
        in_specs=[vmem] * 5,
        out_specs=vmem,
        scratch_shapes=[
            pltpu.VMEM((partner_count, 2, total, 2 * faces), jnp.bfloat16),
            pltpu.VMEM((partner_count, total, 2 * faces), jnp.bfloat16),
            pltpu.VMEM((total, faces), jnp.float32),
            pltpu.VMEM((ROWS, total), jnp.float32),
        ],
        compiler_params=params,
    )(packed, columns, weight, mortar_parts, turned_parts)
    returned = lax.all_to_all(summed, ("vol", "rep"), 0, 0, tiled=True)

    pieces = pl.pallas_call(
        functools.partial(back_kernel, rep_count, share),
        out_shape=array(rep_count, slab * share, faces),
        in_specs=[vmem, vmem],
        out_specs=vmem,
        compiler_params=params,
    )(back_mix, returned)
    pieces = exchange([pieces[d] for d in range(rep_count)])
    out = jnp.zeros((blocks * share, faces), jnp.float32)
    for d in range(rep_count):
        out = lax.dynamic_update_slice_in_dim(out, pieces[d], (rep_index ^ d) * slab * share, 0)
    return out.reshape(blocks, share, faces)


def routed_local(surface_state, direction, stiffness, partners, contact_owner, projection, mortar):
    highest = lax.Precision.HIGHEST
    vol_count = lax.axis_size("vol")
    rep_index = lax.axis_index("rep")
    vol_index = lax.axis_index("vol")
    blocks, channel_share, face_count = surface_state.shape
    partner_count = partners.shape[1]
    capacity = max(2, (2 * blocks + vol_count - 1) // vol_count)
    slot_count = vol_count * capacity
    my_columns = lax.dynamic_slice_in_dim(projection, rep_index * channel_share, channel_share, 1)
    my_rows = lax.dynamic_slice_in_dim(projection, rep_index * channel_share, channel_share, 0)

    def fold_one(piece):
        return jnp.einsum("ij,bjf->bif", my_rows, piece, precision=highest)

    counter = jnp.arange(blocks, dtype=jnp.int32)
    same_owner = contact_owner[:, None] == contact_owner[None, :]
    earlier = counter[:, None] < counter[None, :]
    bucket_rank = jnp.sum((same_owner & earlier).astype(jnp.int32), axis=0)
    slot_of = contact_owner * capacity + bucket_rank
    slot_iota = jnp.arange(slot_count, dtype=jnp.int32)
    matches = slot_iota[:, None] == slot_of[None, :]
    occupied = jnp.any(matches, axis=1).astype(jnp.float32)
    source_row = jnp.sum(jnp.where(matches, counter[None, :], 0), axis=1)
    global_ids = vol_index * blocks + counter
    labels = jnp.concatenate([(global_ids + 1)[:, None], partners], axis=1).astype(jnp.float32)
    send_stiff = (stiffness[source_row] * occupied[:, None]).reshape(
        vol_count, capacity, face_count
    )
    send_labels = (labels[source_row] * occupied[:, None]).reshape(
        vol_count, capacity, partner_count + 1
    )

    def pack(values):
        return (values[source_row] * occupied[:, None, None]).reshape(
            vol_count, capacity, channel_share, face_count
        )

    projected = fold_one(lax.all_gather(surface_state, "rep", axis=1, tiled=True))
    moving = fold_one(lax.all_gather(direction, "rep", axis=1, tiled=True))
    received = (
        lax.all_to_all(pack(projected), "vol", split_axis=0, concat_axis=0, tiled=True),
        lax.all_to_all(pack(moving), "vol", split_axis=0, concat_axis=0, tiled=True),
        lax.all_to_all(send_stiff, "vol", split_axis=0, concat_axis=0, tiled=True),
        lax.all_to_all(send_labels, "vol", split_axis=0, concat_axis=0, tiled=True),
    )
    got_state = received[0].reshape(slot_count, channel_share, face_count)
    got_move = received[1].reshape(slot_count, channel_share, face_count)
    got_stiff = received[2].reshape(slot_count, face_count)
    got_labels = received[3].reshape(slot_count, partner_count + 1).astype(jnp.int32)
    slot_ids = got_labels[:, 0] - 1
    partner_ids = got_labels[:, 1:]
    partner_source = partner_ids // blocks
    candidates = slot_ids.reshape(vol_count, capacity)[partner_source]
    offsets = jnp.arange(capacity, dtype=jnp.int32)
    matched = candidates == partner_ids[..., None]
    found = jnp.any(matched, axis=2).astype(jnp.float32)
    partner_offset = jnp.sum(jnp.where(matched, offsets, 0), axis=2)
    partner_slot = partner_source * capacity + partner_offset
    mapped_state = jnp.einsum("rcf,kfg->krcg", got_state, mortar, precision=highest)
    weights = []
    for column in range(partner_count):
        target = partner_slot[:, column]
        contact_gap = got_state - mapped_state[column][target]
        squashed = jax.nn.sigmoid(sharpness * contact_gap)
        weights.append(
            found[:, column][:, None, None]
            * got_stiff[:, None, :]
            * sharpness
            * squashed
            * (1.0 - squashed)
        )
    partner_slot, weights = (partner_slot, weights)
    mapped_move = jnp.einsum("rcf,kfg->krcg", got_move, mortar, precision=highest)
    tangent = jnp.zeros_like(got_move)
    returns = []
    for column in range(partner_count):
        target = partner_slot[:, column]
        traction = weights[column] * (got_move - mapped_move[column][target])
        tangent = tangent + traction
        returns.append(jax.ops.segment_sum(traction, target, num_segments=slot_count))
    returned = jnp.einsum("krcg,kfg->rcf", jnp.stack(returns), mortar, precision=highest)
    summed = (tangent - returned).reshape(vol_count, capacity, channel_share, face_count)
    returned_tiles = lax.all_to_all(summed, "vol", split_axis=0, concat_axis=0, tiled=True)
    own_tangent = returned_tiles.reshape(slot_count, channel_share, face_count)[slot_of]
    return jnp.einsum(
        "ji,bjf->bif",
        my_columns,
        lax.all_gather(own_tangent, "rep", axis=1, tiled=True),
        precision=highest,
    )


def one_channel_each(mesh, state_shape, partner_shape):
    vol_count, rep_count = mesh.shape["vol"], mesh.shape["rep"]
    total, channels, faces = state_shape
    blocks = total // vol_count
    powers = all(n & (n - 1) == 0 for n in (vol_count, rep_count))
    return (
        powers
        and channels == vol_count * rep_count
        and channels // rep_count == ROWS
        and faces == LANES
        and blocks <= faces
        and blocks % (ROWS // 2 * rep_count) == 0
        and blocks % (2 * ROWS) == 0
        and min(vol_count, rep_count) > 1
        and total % LANES == 0
        and partner_shape[1] < ROWS
    )


def solution(mesh):
    placed = (
        P("vol", "rep", None),
        P("vol", "rep", None),
        P("vol", None),
        P("vol", None),
        P("vol"),
        P(),
        P(),
    )

    def program(surface_state, direction, stiffness, partners, *rest):
        fits = one_channel_each(mesh, surface_state.shape, partners.shape)
        plan = spread_local if fits else routed_local
        return jax.shard_map(
            plan, mesh=mesh, in_specs=placed, out_specs=P("vol", "rep", None), check_vma=False
        )(surface_state, direction, stiffness, partners, *rest)

    return program
```

```python
import functools

import jax
import jax.numpy as jnp
from jax import lax
from jax.experimental import pallas as pl
from jax.experimental.pallas import tpu as pltpu
from jax.sharding import PartitionSpec as P

sharpness = 1.5
LANES = 128
ROWS = 8


def halves(value):
    high = value.astype(jnp.bfloat16)
    low = (value - high.astype(jnp.float32)).astype(jnp.bfloat16)
    return high, low


def product(a, b):
    return jnp.dot(a, b, preferred_element_type=jnp.float32)


def product3(a, b):
    return product(a[0], b[0]) + product(a[1], b[0]) + product(a[0], b[1])


def three_parts(value):
    high, low = halves(value)
    return high, high, low


def iota(shape, dim):
    return lax.broadcasted_iota(jnp.int32, shape, dim)


def one_where(cond):
    return jnp.where(cond, 1.0, 0.0).astype(jnp.bfloat16)


def mixer(projection, channel_of, height, rep_index, rep_count, share, group):
    channels = projection.shape[0]
    width = rep_count * group * share
    place = iota((height, channels), 0) // group
    spread = one_where(channel_of(place) == iota((height, channels), 1))
    col = iota((channels, width), 1)
    j = (rep_index ^ (col // (group * share))) * share + col % share
    pick = one_where(iota((channels, width), 0) == j)
    keep = iota((height, width), 0) % group == (iota((height, width), 1) // share) % group
    out = []
    for part in halves(projection):
        wide = product(product(spread, part).astype(jnp.bfloat16), pick)
        out.append(jnp.where(keep, wide, 0.0).astype(jnp.bfloat16))
    return out


def back_mixer_kernel(rep_count, share, places_ref, projection_ref, after_ref, mix_ref):
    projection, rep_index = projection_ref[...], places_ref[1]
    parts = mixer(projection, lambda i: i, mix_ref.shape[2], rep_index, rep_count, share, ROWS)
    for at, part in enumerate(parts):
        mix_ref[at] = part.astype(jnp.float32).T.astype(jnp.bfloat16)


def project_state_kernel(share, slab, places_ref, projection_ref, labels_ref, *refs):
    slab_refs, out_ref = refs[:-1], refs[-1]
    channels, padded, faces = out_ref.shape
    rep_count = len(slab_refs)
    mix = mixer(projection_ref[...], lambda i: i, channels * ROWS, places_ref[1], rep_count, share, ROWS)
    count = labels_ref.shape[0]
    spare = jnp.zeros((padded - slab - count, faces), jnp.float32)
    tail = jnp.concatenate([labels_ref[...], spare], axis=0) if spare.shape[0] else labels_ref[...]
    for b in range(0, slab, ROWS):
        count = min(ROWS, slab - b)
        pieces = []
        for ref in slab_refs:
            pieces.append(ref[pl.ds(b * share, count * share), :])
            if count < ROWS:
                pieces.append(jnp.zeros(((ROWS - count) * share, faces), jnp.float32))
        out = product3(mix, halves(jnp.concatenate(pieces, axis=0))).reshape(channels, ROWS, faces)
        out_ref[:, pl.ds(b, count), :] = out[:, :count]
    out_ref[:, slab:padded, :] = jnp.broadcast_to(tail[None], (channels, padded - slab, faces))


def project_move_kernel(rep_count, share, places_ref, projection_ref, *refs):
    in_refs, out_refs = refs[:rep_count], refs[rep_count:]
    blocks, faces = out_refs[0].shape
    per = ROWS * share
    me, rep_index = places_ref[0], places_ref[1]

    def channel_of(d):
        return (me ^ d) * rep_count + rep_index

    mix = mixer(projection_ref[...], channel_of, len(out_refs) * ROWS, rep_index, rep_count, share, ROWS)
    groups = blocks // ROWS
    for g in range(0, groups, 2):
        pair = range(g, min(g + 2, groups))
        wide = [jnp.concatenate([ref[pl.ds(p * per, per), :] for ref in in_refs], axis=0) for p in pair]
        out = product3(mix, halves(jnp.concatenate(wide, axis=1)))
        for at, p in enumerate(pair):
            for d, out_ref in enumerate(out_refs):
                out_ref[pl.ds(p * ROWS, ROWS), :] = out[d * ROWS : (d + 1) * ROWS, at * faces : (at + 1) * faces]


def back_kernel(rep_count, share, mix_ref, summed_ref, out_ref):
    channels, padded, faces = summed_ref.shape
    size = channels * ROWS
    mix = mix_ref[0], mix_ref[1]
    rows = out_ref.shape[1]
    for b in range(0, padded, ROWS):
        values = halves(summed_ref[:, pl.ds(b, ROWS), :].reshape(size, faces))
        out = product3(mix, values).reshape(rep_count, ROWS * share, faces)
        count = min(ROWS * share, rows - b * share)
        out_ref[:, pl.ds(b * share, count), :] = out[:, :count]


def map_parts(values, partner_count, faces, info_ref, maps_ref, mapped_ref):
    for k in range(partner_count):
        mortar = info_ref[partner_count + 1, k * faces : (k + 1) * faces, :]
        for at, part in enumerate(three_parts(mortar)):
            maps_ref[at * faces : (at + 1) * faces, k * faces : (k + 1) * faces] = part
    high, low = halves(values)
    mapped = product(jnp.concatenate([high, low, high], axis=1), maps_ref[...])
    for k in range(partner_count):
        high, low = halves(mapped[:, k * faces : (k + 1) * faces])
        mapped_ref[k, :, :faces] = high
        mapped_ref[k, :, faces:] = low


def one_hot(k, r, rows, partner_count, info_ref):
    column = info_ref[partner_count, pl.ds(r, rows), k : k + 1]
    return one_where(iota((rows, info_ref.shape[1]), 1).astype(jnp.float32) == column)


def gather(hot, mapped):
    faces = mapped.shape[1] // 2
    parts = product(hot, mapped)
    return parts[:, :faces] + parts[:, faces:]


def in_turn(tiles, ahead, first, then):
    made = {at: first(*tiles[at]) for at in range(min(ahead, len(tiles)))}
    for at, tile in enumerate(tiles):
        if at + ahead < len(tiles):
            made[at + ahead] = first(*tiles[at + ahead])
        then(*tile, made.pop(at))


def slope_kernel(rep_count, slab, packed_ref, mortar_ref, info_ref, state_ref, maps_ref, mapped_ref, labels_ref, arrived):
    planes, total, faces = info_ref.shape
    partner_count = planes - 2
    devices = packed_ref.shape[0]
    blocks = slab * rep_count
    taken = ROWS // rep_count
    copy = pltpu.make_async_copy(
        mortar_ref, info_ref.at[partner_count + 1, pl.ds(0, partner_count * faces)], arrived
    )
    copy.start()
    for device in range(devices):
        state_ref[device * slab : (device + 1) * slab, :] = packed_ref[device, 0:slab, :]
    labels_ref[...] = jnp.zeros_like(labels_ref)
    for vol in range(devices // rep_count):
        for rep in range(rep_count):
            row = rep * taken
            labels_ref[row : row + taken, :] = packed_ref[vol * rep_count + rep, slab : slab + taken, :]
        info_ref[partner_count, vol * blocks : (vol + 1) * blocks, :] = labels_ref[...].T[:blocks]
    owner_column = info_ref[partner_count, :, partner_count : partner_count + 1]
    owners = jnp.broadcast_to(owner_column, (total, faces))
    small_owners = owners.astype(jnp.bfloat16)
    copy.wait()
    map_parts(state_ref[...], partner_count, faces, info_ref, maps_ref, mapped_ref)
    rows = total // 2

    def first(k, r):
        hot = one_hot(k, r, rows, partner_count, info_ref)
        return gather(hot, mapped_ref[k]), product(hot, small_owners)

    def then(k, r, made):
        gathered, partner_owner = made
        span = pl.ds(r, rows)
        agree = partner_owner == info_ref[partner_count, span, partner_count : partner_count + 1]
        small = jnp.exp(-sharpness * jnp.abs(state_ref[span, :] - gathered))
        slope = sharpness * small / ((1.0 + small) * (1.0 + small))
        info_ref[k, span, :] = jnp.where(agree, slope, 0.0)

    tiles = [(k, r) for k in range(partner_count) for r in range(0, total, rows)]
    in_turn(tiles, 2, first, then)


def contact_kernel(order, places_ref, stiffness_ref, info_ref, *refs):
    swaps = len(order)
    piece_refs, refs = refs[:swaps], refs[swaps:]
    out_ref, move_ref, stiff_ref, maps_ref, turned_maps_ref, mapped_ref, back_ref, tangent_ref, rows_ref = refs
    total, faces = tangent_ref.shape
    partner_count = info_ref.shape[0] - 2
    blocks = total // swaps
    half = blocks // 2
    rows = total // 2
    for at, d in enumerate(order):
        start = pl.multiple_of((places_ref[0] ^ d) * blocks, ROWS)
        move_ref[pl.ds(start, blocks), :] = piece_refs[d][...]
        for side in range(2):
            first = pl.multiple_of(start + (places_ref[1] % 2 ^ side) * half, ROWS)
            stiff_ref[pl.ds(first, half), :] = stiffness_ref[side, at]
    map_parts(move_ref[...], partner_count, faces, info_ref, maps_ref, mapped_ref)
    for k in range(partner_count):
        mortar = info_ref[partner_count + 1, k * faces : (k + 1) * faces, :]
        for at, part in enumerate(three_parts(mortar.T)):
            turned_maps_ref[k, at * faces : (at + 1) * faces, :] = part
    for t in range(0, total, LANES):
        rows_ref[:, t : t + LANES] = info_ref[partner_count, t : t + LANES, :].T[:ROWS]
    waiting = []

    def send_back(k, r, parts):
        high, low = halves(product(parts, turned_maps_ref[k]))
        back_ref[k, pl.ds(r, rows), :faces] = high
        back_ref[k, pl.ds(r, rows), faces:] = low

    def then(k, r, gathered):
        span = pl.ds(r, rows)
        traction = stiff_ref[span, :] * info_ref[k, span, :] * (move_ref[span, :] - gathered)
        if k == 0:
            tangent_ref[span, :] = traction
        else:
            tangent_ref[span, :] += traction
        high, low = halves(traction)
        if waiting:
            send_back(*waiting.pop())
        waiting.append((k, r, jnp.concatenate([high, low, high], axis=1)))

    tiles = [(k, r) for k in range(partner_count) for r in range(0, total, rows)]
    in_turn(tiles, 2, lambda k, r: gather(one_hot(k, r, rows, partner_count, info_ref), mapped_ref[k]), then)
    send_back(*waiting.pop())

    def turned(k, r):
        return one_where((iota((rows, total), 0) + r).astype(jnp.float32) == rows_ref[k : k + 1, :])

    for r in range(0, total, rows):
        span = pl.ds(r, rows)
        back = product(turned(0, r), back_ref[0])
        for k in range(1, partner_count):
            back += product(turned(k, r), back_ref[k])
        tangent_ref[span, :] = tangent_ref[span, :] - back[:, :faces] - back[:, faces:]
    devices, padded, _ = out_ref.shape
    slab = total // devices
    for device in range(devices):
        out_ref[device, 0:slab, :] = tangent_ref[device * slab : (device + 1) * slab, :]
        if padded > slab:
            out_ref[device, slab:padded, :] = jnp.zeros((padded - slab, faces), jnp.float32)


def spread_local(surface_state, direction, stiffness, partners, contact_owner, projection, mortar):
    vol_count, rep_count = lax.axis_size("vol"), lax.axis_size("rep")
    devices = vol_count * rep_count
    vol_index, rep_index = lax.axis_index("vol"), lax.axis_index("rep")
    blocks, share, faces = surface_state.shape
    channels = projection.shape[0]
    partner_count = partners.shape[1]
    slab = blocks // rep_count
    padded = -(-slab // ROWS) * ROWS
    total = blocks * vol_count
    size = channels * ROWS
    vmem = pl.BlockSpec(memory_space=pltpu.VMEM)
    smem = pl.BlockSpec(memory_space=pltpu.SMEM)
    params = pltpu.CompilerParams(vmem_limit_bytes=18 * 1024 * 1024)
    places = jnp.stack([vol_index, rep_index]).astype(jnp.int32)

    def array(*shape, dtype=jnp.float32):
        return jax.ShapeDtypeStruct(shape, dtype)

    def scratch(*shape, dtype=jnp.float32):
        return pltpu.VMEM(shape, dtype)

    def swap(value, axis, d):
        count = lax.axis_size(axis)
        return lax.ppermute(value, axis, [(i, i ^ d) for i in range(count)])

    def exchange(pieces):
        return pieces[:1] + [swap(pieces[d], "rep", d) for d in range(1, rep_count)]

    state = exchange([
        lax.dynamic_slice_in_dim(surface_state, (rep_index ^ d) * slab, slab, 0).reshape(slab * share, faces)
        for d in range(rep_count)
    ])

    state[rep_count // 2], direction = lax.optimization_barrier((state[rep_count // 2], direction))

    move = {0: direction.reshape(blocks * share, faces)}
    step = rep_count // 2
    while step:
        move.update({d ^ step: swap(value, "rep", step) for d, value in move.items()})
        step //= 2

    half = blocks // 2
    stiffness = lax.dynamic_slice_in_dim(stiffness, rep_index % 2 * half, half, 0)
    stiffness = jnp.stack([stiffness, swap(stiffness, "vol", 1)])
    far = list(range(2, vol_count, 2))
    order = [d ^ near for d in [0] + far for near in range(2)]
    stiffness = [stiffness] + [swap(stiffness, "vol", d) for d in far]

    taken = ROWS // rep_count
    labels = jnp.concatenate([partners.T, contact_owner[None, :]], axis=0).astype(jnp.float32)
    labels = jnp.pad(labels, ((0, ROWS - partner_count - 1), (0, faces - blocks)))
    labels = lax.dynamic_slice_in_dim(labels, rep_index * taken, taken, 0)

    sent = pl.pallas_call(
        functools.partial(project_state_kernel, share, slab),
        out_shape=array(channels, padded, faces),
        in_specs=[smem] + [vmem] * (2 + rep_count),
        out_specs=vmem,
        compiler_params=params,
    )(places, projection, labels, *state)
    sent, stiffness = lax.optimization_barrier((sent, stiffness))
    packed = lax.all_to_all(sent, ("vol", "rep"), 0, 0, tiled=True)

    stiffness = jnp.concatenate(stiffness, axis=0)
    stiffness = jnp.stack([stiffness, swap(stiffness, "rep", 1)])
    move, stiffness = lax.optimization_barrier((move, stiffness))
    moved = list(pl.pallas_call(
        functools.partial(project_move_kernel, rep_count, share),
        out_shape=(array(blocks, faces),) * vol_count,
        in_specs=[smem] + [vmem] * (1 + rep_count),
        out_specs=(vmem,) * vol_count,
        compiler_params=params,
    )(places, projection, *[move[d] for d in range(rep_count)]))
    moved = [swap(piece, "vol", d) if d else piece for d, piece in enumerate(moved)]

    info = pl.pallas_call(
        functools.partial(slope_kernel, rep_count, slab),
        out_shape=array(partner_count + 2, total, faces),
        in_specs=[vmem, pl.BlockSpec(memory_space=pl.ANY)],
        out_specs=vmem,
        scratch_shapes=[
            scratch(total, faces),
            scratch(3 * faces, partner_count * faces, dtype=jnp.bfloat16),
            scratch(partner_count, total, 2 * faces, dtype=jnp.bfloat16),
            scratch(LANES, LANES),
            pltpu.SemaphoreType.DMA,
        ],
        compiler_params=params,
    )(packed, mortar.reshape(partner_count * faces, faces))

    summed = pl.pallas_call(
        functools.partial(contact_kernel, tuple(order)),
        out_shape=array(devices, padded, faces),
        in_specs=[smem] + [vmem] * (2 + vol_count),
        out_specs=vmem,
        scratch_shapes=[
            scratch(total, faces),
            scratch(total, faces),
            scratch(3 * faces, partner_count * faces, dtype=jnp.bfloat16),
            scratch(partner_count, 3 * faces, faces, dtype=jnp.bfloat16),
            scratch(partner_count, total, 2 * faces, dtype=jnp.bfloat16),
            scratch(partner_count, total, 2 * faces, dtype=jnp.bfloat16),
            scratch(total, faces),
            scratch(ROWS, total),
        ],
        compiler_params=params,
    )(places, stiffness, info, *moved)
    summed, after = lax.optimization_barrier((summed, places))
    back_mix = pl.pallas_call(
        functools.partial(back_mixer_kernel, rep_count, share),
        out_shape=array(2, size, size, dtype=jnp.bfloat16),
        in_specs=[smem, vmem, smem],
        out_specs=vmem,
        compiler_params=params,
    )(places, projection, after)
    returned = lax.all_to_all(summed, ("vol", "rep"), 0, 0, tiled=True)

    pieces = pl.pallas_call(
        functools.partial(back_kernel, rep_count, share),
        out_shape=array(rep_count, slab * share, faces),
        in_specs=[vmem, vmem],
        out_specs=vmem,
        compiler_params=params,
    )(back_mix, returned)
    pieces = exchange([pieces[d] for d in range(rep_count)])
    out = jnp.zeros((blocks * share, faces), jnp.float32)
    for d in range(rep_count):
        out = lax.dynamic_update_slice_in_dim(out, pieces[d], (rep_index ^ d) * slab * share, 0)
    return out.reshape(blocks, share, faces)


def routed_local(surface_state, direction, stiffness, partners, contact_owner, projection, mortar):
    highest = lax.Precision.HIGHEST
    vol_count = lax.axis_size("vol")
    rep_index = lax.axis_index("rep")
    vol_index = lax.axis_index("vol")
    blocks, channel_share, face_count = surface_state.shape
    partner_count = partners.shape[1]
    capacity = max(2, (2 * blocks + vol_count - 1) // vol_count)
    slot_count = vol_count * capacity
    my_columns = lax.dynamic_slice_in_dim(projection, rep_index * channel_share, channel_share, 1)
    my_rows = lax.dynamic_slice_in_dim(projection, rep_index * channel_share, channel_share, 0)

    def fold_one(piece):
        return jnp.einsum("ij,bjf->bif", my_rows, piece, precision=highest)

    counter = jnp.arange(blocks, dtype=jnp.int32)
    same_owner = contact_owner[:, None] == contact_owner[None, :]
    earlier = counter[:, None] < counter[None, :]
    bucket_rank = jnp.sum((same_owner & earlier).astype(jnp.int32), axis=0)
    slot_of = contact_owner * capacity + bucket_rank
    slot_iota = jnp.arange(slot_count, dtype=jnp.int32)
    matches = slot_iota[:, None] == slot_of[None, :]
    occupied = jnp.any(matches, axis=1).astype(jnp.float32)
    source_row = jnp.sum(jnp.where(matches, counter[None, :], 0), axis=1)
    global_ids = vol_index * blocks + counter
    labels = jnp.concatenate([(global_ids + 1)[:, None], partners], axis=1).astype(jnp.float32)
    send_stiff = (stiffness[source_row] * occupied[:, None]).reshape(
        vol_count, capacity, face_count
    )
    send_labels = (labels[source_row] * occupied[:, None]).reshape(
        vol_count, capacity, partner_count + 1
    )

    def pack(values):
        return (values[source_row] * occupied[:, None, None]).reshape(
            vol_count, capacity, channel_share, face_count
        )

    projected = fold_one(lax.all_gather(surface_state, "rep", axis=1, tiled=True))
    moving = fold_one(lax.all_gather(direction, "rep", axis=1, tiled=True))
    received = (
        lax.all_to_all(pack(projected), "vol", split_axis=0, concat_axis=0, tiled=True),
        lax.all_to_all(pack(moving), "vol", split_axis=0, concat_axis=0, tiled=True),
        lax.all_to_all(send_stiff, "vol", split_axis=0, concat_axis=0, tiled=True),
        lax.all_to_all(send_labels, "vol", split_axis=0, concat_axis=0, tiled=True),
    )
    got_state = received[0].reshape(slot_count, channel_share, face_count)
    got_move = received[1].reshape(slot_count, channel_share, face_count)
    got_stiff = received[2].reshape(slot_count, face_count)
    got_labels = received[3].reshape(slot_count, partner_count + 1).astype(jnp.int32)
    slot_ids = got_labels[:, 0] - 1
    partner_ids = got_labels[:, 1:]
    partner_source = partner_ids // blocks
    candidates = slot_ids.reshape(vol_count, capacity)[partner_source]
    offsets = jnp.arange(capacity, dtype=jnp.int32)
    matched = candidates == partner_ids[..., None]
    found = jnp.any(matched, axis=2).astype(jnp.float32)
    partner_offset = jnp.sum(jnp.where(matched, offsets, 0), axis=2)
    partner_slot = partner_source * capacity + partner_offset
    mapped_state = jnp.einsum("rcf,kfg->krcg", got_state, mortar, precision=highest)
    weights = []
    for column in range(partner_count):
        target = partner_slot[:, column]
        contact_gap = got_state - mapped_state[column][target]
        squashed = jax.nn.sigmoid(sharpness * contact_gap)
        weights.append(
            found[:, column][:, None, None]
            * got_stiff[:, None, :]
            * sharpness
            * squashed
            * (1.0 - squashed)
        )
    partner_slot, weights = (partner_slot, weights)
    mapped_move = jnp.einsum("rcf,kfg->krcg", got_move, mortar, precision=highest)
    tangent = jnp.zeros_like(got_move)
    returns = []
    for column in range(partner_count):
        target = partner_slot[:, column]
        traction = weights[column] * (got_move - mapped_move[column][target])
        tangent = tangent + traction
        returns.append(jax.ops.segment_sum(traction, target, num_segments=slot_count))
    returned = jnp.einsum("krcg,kfg->rcf", jnp.stack(returns), mortar, precision=highest)
    summed = (tangent - returned).reshape(vol_count, capacity, channel_share, face_count)
    returned_tiles = lax.all_to_all(summed, "vol", split_axis=0, concat_axis=0, tiled=True)
    own_tangent = returned_tiles.reshape(slot_count, channel_share, face_count)[slot_of]
    return jnp.einsum(
        "ji,bjf->bif",
        my_columns,
        lax.all_gather(own_tangent, "rep", axis=1, tiled=True),
        precision=highest,
    )


def one_channel_each(mesh, state_shape, partner_shape):
    vol_count, rep_count = mesh.shape["vol"], mesh.shape["rep"]
    total, channels, faces = state_shape
    blocks = total // vol_count
    powers = all(n & (n - 1) == 0 for n in (vol_count, rep_count))
    return (
        powers
        and channels == vol_count * rep_count
        and channels // rep_count == ROWS
        and faces == LANES
        and blocks <= faces
        and blocks % (ROWS // 2 * rep_count) == 0
        and blocks % (2 * ROWS) == 0
        and ROWS % rep_count == 0
        and -(blocks // rep_count) % ROWS >= ROWS // rep_count
        and min(vol_count, rep_count) > 1
        and total % LANES == 0
        and partner_shape[1] < ROWS
        and partner_shape[1] * LANES <= total
    )


def solution(mesh):
    placed = (
        P("vol", "rep", None),
        P("vol", "rep", None),
        P("vol", None),
        P("vol", None),
        P("vol"),
        P(),
        P(),
    )

    def program(surface_state, direction, stiffness, partners, *rest):
        fits = one_channel_each(mesh, surface_state.shape, partners.shape)
        plan = spread_local if fits else routed_local
        return jax.shard_map(
            plan, mesh=mesh, in_specs=placed, out_specs=P("vol", "rep", None), check_vma=False
        )(surface_state, direction, stiffness, partners, *rest)

    return program
```

```python
import functools

import jax
import jax.numpy as jnp
from jax import lax
from jax.experimental import pallas as pl
from jax.experimental.pallas import tpu as pltpu
from jax.sharding import PartitionSpec as P

sharpness = 1.5
LANES = 128
ROWS = 8


def halves(value):
    high = value.astype(jnp.bfloat16)
    low = (value - high.astype(jnp.float32)).astype(jnp.bfloat16)
    return high, low


def product(a, b):
    return jnp.dot(a, b, preferred_element_type=jnp.float32)


def product3(a, b):
    return product(a[0], b[0]) + product(a[1], b[0]) + product(a[0], b[1])


def three_parts(value):
    high, low = halves(value)
    return high, high, low


def iota(shape, dim):
    return lax.broadcasted_iota(jnp.int32, shape, dim)


def one_where(cond):
    return jnp.where(cond, 1.0, 0.0).astype(jnp.bfloat16)


def starts(slab):
    return [min(b, slab - ROWS) for b in range(0, slab, ROWS)]


def mixer(projection, channel_of, height, rep_index, rep_count, share, group):
    channels = projection.shape[0]
    width = rep_count * group * share
    place = iota((height, channels), 0) // group
    spread = one_where(channel_of(place) == iota((height, channels), 1))
    col = iota((channels, width), 1)
    j = (rep_index ^ (col // (group * share))) * share + col % share
    pick = one_where(iota((channels, width), 0) == j)
    keep = iota((height, width), 0) % group == (iota((height, width), 1) // share) % group
    out = []
    for part in halves(projection):
        wide = product(product(spread, part).astype(jnp.bfloat16), pick)
        out.append(jnp.where(keep, wide, 0.0).astype(jnp.bfloat16))
    return out


def back_mixer_kernel(rep_count, share, places_ref, projection_ref, after_ref, mix_ref):
    projection, rep_index = projection_ref[...], places_ref[1]
    parts = mixer(projection, lambda i: i, mix_ref.shape[2], rep_index, rep_count, share, ROWS)
    for at, part in enumerate(parts):
        mix_ref[at] = part.astype(jnp.float32).T.astype(jnp.bfloat16)


def state_mixer_kernel(rep_count, share, places_ref, table_ref, mix_ref):
    channels = table_ref.shape[0] - ROWS
    projection = table_ref[ROWS:, 0:channels]
    parts = mixer(projection, lambda i: i, mix_ref.shape[1], places_ref[1], rep_count, share, ROWS)
    for at, part in enumerate(parts):
        mix_ref[at] = part


def project_state_kernel(share, slab, places_ref, mix_ref, table_ref, *refs):
    slab_refs, out_ref = refs[:-1], refs[-1]
    channels, length, faces = out_ref.shape
    mix = mix_ref[0], mix_ref[1]
    for b in starts(slab):
        pieces = [ref[pl.ds(b * share, ROWS * share), :] for ref in slab_refs]
        out = product3(mix, halves(jnp.concatenate(pieces, axis=0))).reshape(channels, ROWS, faces)
        out_ref[:, pl.ds(b, ROWS), :] = out
    tail = table_ref[pl.ds(places_ref[1] * (length - slab), length - slab), :]
    out_ref[:, slab:length, :] = jnp.broadcast_to(tail[None], (channels,) + tail.shape)


def project_move_kernel(rep_count, share, places_ref, projection_ref, *refs):
    in_refs, out_refs = refs[:rep_count], refs[rep_count:]
    blocks, faces = out_refs[0].shape
    per = ROWS * share
    me, rep_index = places_ref[0], places_ref[1]

    def channel_of(d):
        return (me ^ d) * rep_count + rep_index

    mix = mixer(projection_ref[...], channel_of, len(out_refs) * ROWS, rep_index, rep_count, share, ROWS)
    groups = blocks // ROWS
    for g in range(0, groups, 2):
        pair = range(g, min(g + 2, groups))
        wide = [jnp.concatenate([ref[pl.ds(p * per, per), :] for ref in in_refs], axis=0) for p in pair]
        out = product3(mix, halves(jnp.concatenate(wide, axis=1)))
        for at, p in enumerate(pair):
            for d, out_ref in enumerate(out_refs):
                out_ref[pl.ds(p * ROWS, ROWS), :] = out[d * ROWS : (d + 1) * ROWS, at * faces : (at + 1) * faces]


def back_kernel(rep_count, share, mix_ref, summed_ref, out_ref):
    channels, slab, faces = summed_ref.shape
    mix = mix_ref[0], mix_ref[1]
    for b in starts(slab):
        values = halves(summed_ref[:, pl.ds(b, ROWS), :].reshape(channels * ROWS, faces))
        out = product3(mix, values).reshape(rep_count, ROWS * share, faces)
        out_ref[:, pl.ds(b * share, ROWS * share), :] = out


def map_parts(values, partner_count, faces, info_ref, maps_ref, mapped_ref):
    for k in range(partner_count):
        mortar = info_ref[partner_count + 1, k * faces : (k + 1) * faces, :]
        for at, part in enumerate(three_parts(mortar)):
            maps_ref[at * faces : (at + 1) * faces, k * faces : (k + 1) * faces] = part
    high, low = halves(values)
    mapped = product(jnp.concatenate([high, low, high], axis=1), maps_ref[...])
    for k in range(partner_count):
        high, low = halves(mapped[:, k * faces : (k + 1) * faces])
        mapped_ref[k, :, :faces] = high
        mapped_ref[k, :, faces:] = low


def one_hot(k, r, rows, partner_count, info_ref):
    column = info_ref[partner_count, pl.ds(r, rows), k : k + 1]
    return one_where(iota((rows, info_ref.shape[1]), 1).astype(jnp.float32) == column)


def gather(hot, mapped):
    faces = mapped.shape[1] // 2
    parts = product(hot, mapped)
    return parts[:, :faces] + parts[:, faces:]


def in_turn(tiles, ahead, first, then):
    made = {at: first(*tiles[at]) for at in range(min(ahead, len(tiles)))}
    for at, tile in enumerate(tiles):
        if at + ahead < len(tiles):
            made[at + ahead] = first(*tiles[at + ahead])
        then(*tile, made.pop(at))


def slope_kernel(rep_count, slab, packed_ref, mortar_ref, info_ref, state_ref, maps_ref, mapped_ref, labels_ref, arrived):
    planes, total, faces = info_ref.shape
    partner_count = planes - 2
    devices = packed_ref.shape[0]
    blocks = slab * rep_count
    taken = ROWS // rep_count
    copy = pltpu.make_async_copy(
        mortar_ref, info_ref.at[partner_count + 1, pl.ds(0, partner_count * faces)], arrived
    )
    copy.start()
    for device in range(devices):
        state_ref[device * slab : (device + 1) * slab, :] = packed_ref[device, 0:slab, :]
    labels_ref[...] = jnp.zeros_like(labels_ref)
    for vol in range(devices // rep_count):
        for rep in range(rep_count):
            row = rep * taken
            labels_ref[row : row + taken, :] = packed_ref[vol * rep_count + rep, slab : slab + taken, :]
        info_ref[partner_count, vol * blocks : (vol + 1) * blocks, :] = labels_ref[...].T[:blocks]
    owner_column = info_ref[partner_count, :, partner_count : partner_count + 1]
    owners = jnp.broadcast_to(owner_column, (total, faces))
    small_owners = owners.astype(jnp.bfloat16)
    copy.wait()
    map_parts(state_ref[...], partner_count, faces, info_ref, maps_ref, mapped_ref)
    rows = total // 2

    def first(k, r):
        hot = one_hot(k, r, rows, partner_count, info_ref)
        return gather(hot, mapped_ref[k]), product(hot, small_owners)

    def then(k, r, made):
        gathered, partner_owner = made
        span = pl.ds(r, rows)
        agree = partner_owner == info_ref[partner_count, span, partner_count : partner_count + 1]
        small = jnp.exp(-sharpness * jnp.abs(state_ref[span, :] - gathered))
        slope = sharpness * small / ((1.0 + small) * (1.0 + small))
        info_ref[k, span, :] = jnp.where(agree, slope, 0.0)

    tiles = [(k, r) for k in range(partner_count) for r in range(0, total, rows)]
    in_turn(tiles, 2, first, then)


def contact_kernel(order, places_ref, stiffness_ref, info_ref, *refs):
    swaps = len(order)
    piece_refs, refs = refs[:swaps], refs[swaps:]
    out_ref, move_ref, stiff_ref, maps_ref, turned_maps_ref, mapped_ref, back_ref, tangent_ref, rows_ref = refs
    total, faces = tangent_ref.shape
    partner_count = info_ref.shape[0] - 2
    blocks = total // swaps
    half = blocks // 2
    rows = total // 2
    for at, d in enumerate(order):
        start = pl.multiple_of((places_ref[0] ^ d) * blocks, ROWS)
        move_ref[pl.ds(start, blocks), :] = piece_refs[d][...]
        for side in range(2):
            first = pl.multiple_of(start + (places_ref[1] % 2 ^ side) * half, ROWS)
            stiff_ref[pl.ds(first, half), :] = stiffness_ref[side, at]
    map_parts(move_ref[...], partner_count, faces, info_ref, maps_ref, mapped_ref)
    for k in range(partner_count):
        mortar = info_ref[partner_count + 1, k * faces : (k + 1) * faces, :]
        for at, part in enumerate(three_parts(mortar.T)):
            turned_maps_ref[k, at * faces : (at + 1) * faces, :] = part
    for t in range(0, total, LANES):
        rows_ref[:, t : t + LANES] = info_ref[partner_count, t : t + LANES, :].T[:ROWS]
    waiting = []

    def send_back(k, r, parts):
        high, low = halves(product(parts, turned_maps_ref[k]))
        back_ref[k, pl.ds(r, rows), :faces] = high
        back_ref[k, pl.ds(r, rows), faces:] = low

    def then(k, r, gathered):
        span = pl.ds(r, rows)
        traction = stiff_ref[span, :] * info_ref[k, span, :] * (move_ref[span, :] - gathered)
        if k == 0:
            tangent_ref[span, :] = traction
        else:
            tangent_ref[span, :] += traction
        high, low = halves(traction)
        if waiting:
            send_back(*waiting.pop())
        waiting.append((k, r, jnp.concatenate([high, low, high], axis=1)))

    tiles = [(k, r) for k in range(partner_count) for r in range(0, total, rows)]
    in_turn(tiles, 2, lambda k, r: gather(one_hot(k, r, rows, partner_count, info_ref), mapped_ref[k]), then)
    send_back(*waiting.pop())

    def turned(k, r):
        return one_where((iota((rows, total), 0) + r).astype(jnp.float32) == rows_ref[k : k + 1, :])

    for r in range(0, total, rows):
        span = pl.ds(r, rows)
        back = product(turned(0, r), back_ref[0])
        for k in range(1, partner_count):
            back += product(turned(k, r), back_ref[k])
        tangent_ref[span, :] = tangent_ref[span, :] - back[:, :faces] - back[:, faces:]
    devices, slab, _ = out_ref.shape
    for device in range(devices):
        out_ref[device] = tangent_ref[device * slab : (device + 1) * slab, :]


def spread_local(surface_state, direction, stiffness, partners, contact_owner, projection, mortar):
    vol_count, rep_count = lax.axis_size("vol"), lax.axis_size("rep")
    devices = vol_count * rep_count
    vol_index, rep_index = lax.axis_index("vol"), lax.axis_index("rep")
    blocks, share, faces = surface_state.shape
    channels = projection.shape[0]
    partner_count = partners.shape[1]
    slab = blocks // rep_count
    total = blocks * vol_count
    size = channels * ROWS
    vmem = pl.BlockSpec(memory_space=pltpu.VMEM)
    smem = pl.BlockSpec(memory_space=pltpu.SMEM)
    params = pltpu.CompilerParams(vmem_limit_bytes=18 * 1024 * 1024)
    places = jnp.stack([vol_index, rep_index]).astype(jnp.int32)

    def array(*shape, dtype=jnp.float32):
        return jax.ShapeDtypeStruct(shape, dtype)

    def scratch(*shape, dtype=jnp.float32):
        return pltpu.VMEM(shape, dtype)

    def swap(value, axis, d):
        count = lax.axis_size(axis)
        return lax.ppermute(value, axis, [(i, i ^ d) for i in range(count)])

    def exchange(pieces):
        return pieces[:1] + [swap(pieces[d], "rep", d) for d in range(1, rep_count)]

    state = exchange([
        lax.dynamic_slice_in_dim(surface_state, (rep_index ^ d) * slab, slab, 0).reshape(slab * share, faces)
        for d in range(rep_count)
    ])


    move = {0: direction.reshape(blocks * share, faces)}
    step = rep_count // 2
    while step:
        move.update({d ^ step: swap(value, "rep", step) for d, value in move.items()})
        step //= 2

    half = blocks // 2
    stiffness = lax.dynamic_slice_in_dim(stiffness, rep_index % 2 * half, half, 0)
    stiffness = jnp.stack([stiffness, swap(stiffness, "vol", 1)])
    far = list(range(vol_count - 2, 0, -2))
    order = [d ^ near for d in [0] + far for near in range(2)]
    stiffness, state[0] = lax.optimization_barrier((stiffness, state[0]))
    stiffness = [stiffness] + [swap(stiffness, "vol", d) for d in far]

    taken = ROWS // rep_count
    labels = jnp.concatenate([partners.T, contact_owner[None, :]], axis=0).astype(jnp.float32)
    labels = jnp.pad(labels, ((0, ROWS - partner_count - 1), (0, faces - blocks)))
    table = jnp.concatenate([labels, jnp.pad(projection, ((0, 0), (0, faces - channels)))], axis=0)
    state_mix = pl.pallas_call(
        functools.partial(state_mixer_kernel, rep_count, share),
        out_shape=array(2, size, size, dtype=jnp.bfloat16),
        in_specs=[smem, vmem],
        out_specs=vmem,
        compiler_params=params,
    )(places, table)

    sent = pl.pallas_call(
        functools.partial(project_state_kernel, share, slab),
        out_shape=array(channels, slab + taken, faces),
        in_specs=[smem] + [vmem] * (2 + rep_count),
        out_specs=vmem,
        compiler_params=params,
    )(places, state_mix, table, *state)
    sent, stiffness = lax.optimization_barrier((sent, stiffness))
    packed = lax.all_to_all(sent, ("vol", "rep"), 0, 0, tiled=True)

    stiffness = jnp.concatenate(stiffness, axis=0)
    stiffness = jnp.stack([stiffness, swap(stiffness, "rep", 1)])
    move, stiffness = lax.optimization_barrier((move, stiffness))
    moved = list(pl.pallas_call(
        functools.partial(project_move_kernel, rep_count, share),
        out_shape=(array(blocks, faces),) * vol_count,
        in_specs=[smem] + [vmem] * (1 + rep_count),
        out_specs=(vmem,) * vol_count,
        compiler_params=params,
    )(places, projection, *[move[d] for d in range(rep_count)]))
    moved = [swap(piece, "vol", d) if d else piece for d, piece in enumerate(moved)]

    info = pl.pallas_call(
        functools.partial(slope_kernel, rep_count, slab),
        out_shape=array(partner_count + 2, total, faces),
        in_specs=[vmem, pl.BlockSpec(memory_space=pl.ANY)],
        out_specs=vmem,
        scratch_shapes=[
            scratch(total, faces),
            scratch(3 * faces, partner_count * faces, dtype=jnp.bfloat16),
            scratch(partner_count, total, 2 * faces, dtype=jnp.bfloat16),
            scratch(LANES, LANES),
            pltpu.SemaphoreType.DMA,
        ],
        compiler_params=params,
    )(packed, mortar.reshape(partner_count * faces, faces))

    summed = pl.pallas_call(
        functools.partial(contact_kernel, tuple(order)),
        out_shape=array(devices, slab, faces),
        in_specs=[smem] + [vmem] * (2 + vol_count),
        out_specs=vmem,
        scratch_shapes=[
            scratch(total, faces),
            scratch(total, faces),
            scratch(3 * faces, partner_count * faces, dtype=jnp.bfloat16),
            scratch(partner_count, 3 * faces, faces, dtype=jnp.bfloat16),
            scratch(partner_count, total, 2 * faces, dtype=jnp.bfloat16),
            scratch(partner_count, total, 2 * faces, dtype=jnp.bfloat16),
            scratch(total, faces),
            scratch(ROWS, total),
        ],
        compiler_params=params,
    )(places, stiffness, info, *moved)
    summed, after = lax.optimization_barrier((summed, places))
    back_mix = pl.pallas_call(
        functools.partial(back_mixer_kernel, rep_count, share),
        out_shape=array(2, size, size, dtype=jnp.bfloat16),
        in_specs=[smem, vmem, smem],
        out_specs=vmem,
        compiler_params=params,
    )(places, projection, after)
    returned = lax.all_to_all(summed, ("vol", "rep"), 0, 0, tiled=True)

    pieces = pl.pallas_call(
        functools.partial(back_kernel, rep_count, share),
        out_shape=array(rep_count, slab * share, faces),
        in_specs=[vmem, vmem],
        out_specs=vmem,
        compiler_params=params,
    )(back_mix, returned)
    pieces = exchange([pieces[d] for d in range(rep_count)])
    out = jnp.zeros((blocks * share, faces), jnp.float32)
    for d in range(rep_count):
        out = lax.dynamic_update_slice_in_dim(out, pieces[d], (rep_index ^ d) * slab * share, 0)
    return out.reshape(blocks, share, faces)


def routed_local(surface_state, direction, stiffness, partners, contact_owner, projection, mortar):
    highest = lax.Precision.HIGHEST
    vol_count = lax.axis_size("vol")
    rep_index = lax.axis_index("rep")
    vol_index = lax.axis_index("vol")
    blocks, channel_share, face_count = surface_state.shape
    partner_count = partners.shape[1]
    capacity = max(2, (2 * blocks + vol_count - 1) // vol_count)
    slot_count = vol_count * capacity
    my_columns = lax.dynamic_slice_in_dim(projection, rep_index * channel_share, channel_share, 1)
    my_rows = lax.dynamic_slice_in_dim(projection, rep_index * channel_share, channel_share, 0)

    def fold_one(piece):
        return jnp.einsum("ij,bjf->bif", my_rows, piece, precision=highest)

    counter = jnp.arange(blocks, dtype=jnp.int32)
    same_owner = contact_owner[:, None] == contact_owner[None, :]
    earlier = counter[:, None] < counter[None, :]
    bucket_rank = jnp.sum((same_owner & earlier).astype(jnp.int32), axis=0)
    slot_of = contact_owner * capacity + bucket_rank
    slot_iota = jnp.arange(slot_count, dtype=jnp.int32)
    matches = slot_iota[:, None] == slot_of[None, :]
    occupied = jnp.any(matches, axis=1).astype(jnp.float32)
    source_row = jnp.sum(jnp.where(matches, counter[None, :], 0), axis=1)
    global_ids = vol_index * blocks + counter
    labels = jnp.concatenate([(global_ids + 1)[:, None], partners], axis=1).astype(jnp.float32)
    send_stiff = (stiffness[source_row] * occupied[:, None]).reshape(
        vol_count, capacity, face_count
    )
    send_labels = (labels[source_row] * occupied[:, None]).reshape(
        vol_count, capacity, partner_count + 1
    )

    def pack(values):
        return (values[source_row] * occupied[:, None, None]).reshape(
            vol_count, capacity, channel_share, face_count
        )

    projected = fold_one(lax.all_gather(surface_state, "rep", axis=1, tiled=True))
    moving = fold_one(lax.all_gather(direction, "rep", axis=1, tiled=True))
    received = (
        lax.all_to_all(pack(projected), "vol", split_axis=0, concat_axis=0, tiled=True),
        lax.all_to_all(pack(moving), "vol", split_axis=0, concat_axis=0, tiled=True),
        lax.all_to_all(send_stiff, "vol", split_axis=0, concat_axis=0, tiled=True),
        lax.all_to_all(send_labels, "vol", split_axis=0, concat_axis=0, tiled=True),
    )
    got_state = received[0].reshape(slot_count, channel_share, face_count)
    got_move = received[1].reshape(slot_count, channel_share, face_count)
    got_stiff = received[2].reshape(slot_count, face_count)
    got_labels = received[3].reshape(slot_count, partner_count + 1).astype(jnp.int32)
    slot_ids = got_labels[:, 0] - 1
    partner_ids = got_labels[:, 1:]
    partner_source = partner_ids // blocks
    candidates = slot_ids.reshape(vol_count, capacity)[partner_source]
    offsets = jnp.arange(capacity, dtype=jnp.int32)
    matched = candidates == partner_ids[..., None]
    found = jnp.any(matched, axis=2).astype(jnp.float32)
    partner_offset = jnp.sum(jnp.where(matched, offsets, 0), axis=2)
    partner_slot = partner_source * capacity + partner_offset
    mapped_state = jnp.einsum("rcf,kfg->krcg", got_state, mortar, precision=highest)
    weights = []
    for column in range(partner_count):
        target = partner_slot[:, column]
        contact_gap = got_state - mapped_state[column][target]
        squashed = jax.nn.sigmoid(sharpness * contact_gap)
        weights.append(
            found[:, column][:, None, None]
            * got_stiff[:, None, :]
            * sharpness
            * squashed
            * (1.0 - squashed)
        )
    partner_slot, weights = (partner_slot, weights)
    mapped_move = jnp.einsum("rcf,kfg->krcg", got_move, mortar, precision=highest)
    tangent = jnp.zeros_like(got_move)
    returns = []
    for column in range(partner_count):
        target = partner_slot[:, column]
        traction = weights[column] * (got_move - mapped_move[column][target])
        tangent = tangent + traction
        returns.append(jax.ops.segment_sum(traction, target, num_segments=slot_count))
    returned = jnp.einsum("krcg,kfg->rcf", jnp.stack(returns), mortar, precision=highest)
    summed = (tangent - returned).reshape(vol_count, capacity, channel_share, face_count)
    returned_tiles = lax.all_to_all(summed, "vol", split_axis=0, concat_axis=0, tiled=True)
    own_tangent = returned_tiles.reshape(slot_count, channel_share, face_count)[slot_of]
    return jnp.einsum(
        "ji,bjf->bif",
        my_columns,
        lax.all_gather(own_tangent, "rep", axis=1, tiled=True),
        precision=highest,
    )


def one_channel_each(mesh, state_shape, partner_shape):
    vol_count, rep_count = mesh.shape["vol"], mesh.shape["rep"]
    total, channels, faces = state_shape
    blocks = total // vol_count
    powers = all(n & (n - 1) == 0 for n in (vol_count, rep_count))
    return (
        powers
        and channels == vol_count * rep_count
        and channels // rep_count == ROWS
        and faces == LANES
        and blocks <= faces
        and blocks % (ROWS // 2 * rep_count) == 0
        and blocks % (2 * ROWS) == 0
        and ROWS % rep_count == 0
        and blocks // rep_count >= ROWS
        and min(vol_count, rep_count) > 1
        and total % LANES == 0
        and partner_shape[1] < ROWS
        and partner_shape[1] * LANES <= total
    )


def solution(mesh):
    placed = (
        P("vol", "rep", None),
        P("vol", "rep", None),
        P("vol", None),
        P("vol", None),
        P("vol"),
        P(),
        P(),
    )

    def program(surface_state, direction, stiffness, partners, *rest):
        fits = one_channel_each(mesh, surface_state.shape, partners.shape)
        plan = spread_local if fits else routed_local
        return jax.shard_map(
            plan, mesh=mesh, in_specs=placed, out_specs=P("vol", "rep", None), check_vma=False
        )(surface_state, direction, stiffness, partners, *rest)

    return program
```

```python
import functools

import jax
import jax.numpy as jnp
from jax import lax
from jax.experimental import pallas as pl
from jax.experimental.pallas import tpu as pltpu
from jax.sharding import PartitionSpec as P

sharpness = 1.5
LANES = 128
ROWS = 8


def halves(value):
    high = value.astype(jnp.bfloat16)
    low = (value - high.astype(jnp.float32)).astype(jnp.bfloat16)
    return high, low


def product(a, b):
    return jnp.dot(a, b, preferred_element_type=jnp.float32)


def product3(a, b):
    return product(a[0], b[0]) + product(a[1], b[0]) + product(a[0], b[1])


def three_parts(value):
    high, low = halves(value)
    return high, high, low


def iota(shape, dim):
    return lax.broadcasted_iota(jnp.int32, shape, dim)


def one_where(cond):
    return jnp.where(cond, 1.0, 0.0).astype(jnp.bfloat16)


def starts(slab):
    return [min(b, slab - ROWS) for b in range(0, slab, ROWS)]


def mixer(projection, channel_of, height, rep_index, rep_count, share, group):
    channels = projection.shape[0]
    width = rep_count * group * share
    place = iota((height, channels), 0) // group
    spread = one_where(channel_of(place) == iota((height, channels), 1))
    col = iota((channels, width), 1)
    j = (rep_index ^ (col // (group * share))) * share + col % share
    pick = one_where(iota((channels, width), 0) == j)
    keep = iota((height, width), 0) % group == (iota((height, width), 1) // share) % group
    out = []
    for part in halves(projection):
        wide = product(product(spread, part).astype(jnp.bfloat16), pick)
        out.append(jnp.where(keep, wide, 0.0).astype(jnp.bfloat16))
    return out


def back_mixer_kernel(rep_count, share, places_ref, projection_ref, after_ref, mix_ref):
    projection, rep_index = projection_ref[...], places_ref[1]
    parts = mixer(projection, lambda i: i, mix_ref.shape[2], rep_index, rep_count, share, ROWS)
    for at, part in enumerate(parts):
        mix_ref[at] = part.astype(jnp.float32).T.astype(jnp.bfloat16)


def state_mixer_kernel(rep_count, share, places_ref, table_ref, mix_ref):
    channels = table_ref.shape[0] - ROWS
    projection = table_ref[ROWS:, 0:channels]
    parts = mixer(projection, lambda i: i, mix_ref.shape[1], places_ref[1], rep_count, share, ROWS)
    for at, part in enumerate(parts):
        mix_ref[at] = part


def project_state_kernel(share, slab, places_ref, mix_ref, table_ref, *refs):
    slab_refs, out_ref = refs[:-1], refs[-1]
    channels, length, faces = out_ref.shape
    mix = mix_ref[0], mix_ref[1]
    for b in starts(slab):
        pieces = [ref[pl.ds(b * share, ROWS * share), :] for ref in slab_refs]
        out = product3(mix, halves(jnp.concatenate(pieces, axis=0))).reshape(channels, ROWS, faces)
        out_ref[:, pl.ds(b, ROWS), :] = out
    tail = table_ref[pl.ds(places_ref[1] * (length - slab), length - slab), :]
    out_ref[:, slab:length, :] = jnp.broadcast_to(tail[None], (channels,) + tail.shape)


def project_move_kernel(rep_count, share, places_ref, projection_ref, *refs):
    in_refs, out_refs = refs[:rep_count], refs[rep_count:]
    blocks, faces = out_refs[0].shape
    per = ROWS * share
    me, rep_index = places_ref[0], places_ref[1]

    def channel_of(d):
        return (me ^ d) * rep_count + rep_index

    mix = mixer(projection_ref[...], channel_of, len(out_refs) * ROWS, rep_index, rep_count, share, ROWS)
    groups = blocks // ROWS
    for g in range(0, groups, 2):
        pair = range(g, min(g + 2, groups))
        wide = [jnp.concatenate([ref[pl.ds(p * per, per), :] for ref in in_refs], axis=0) for p in pair]
        out = product3(mix, halves(jnp.concatenate(wide, axis=1)))
        for at, p in enumerate(pair):
            for d, out_ref in enumerate(out_refs):
                out_ref[pl.ds(p * ROWS, ROWS), :] = out[d * ROWS : (d + 1) * ROWS, at * faces : (at + 1) * faces]


def back_kernel(rep_count, share, mix_ref, summed_ref, out_ref):
    channels, slab, faces = summed_ref.shape
    mix = mix_ref[0], mix_ref[1]
    for b in starts(slab):
        values = halves(summed_ref[:, pl.ds(b, ROWS), :].reshape(channels * ROWS, faces))
        out = product3(mix, values).reshape(rep_count, ROWS * share, faces)
        out_ref[:, pl.ds(b * share, ROWS * share), :] = out


def map_parts(values, partner_count, faces, info_ref, maps_ref, mapped_ref):
    for k in range(partner_count):
        mortar = info_ref[partner_count + 1, k * faces : (k + 1) * faces, :]
        for at, part in enumerate(three_parts(mortar)):
            maps_ref[at * faces : (at + 1) * faces, k * faces : (k + 1) * faces] = part
    high, low = halves(values)
    mapped = product(jnp.concatenate([high, low, high], axis=1), maps_ref[...])
    for k in range(partner_count):
        high, low = halves(mapped[:, k * faces : (k + 1) * faces])
        mapped_ref[k, :, :faces] = high
        mapped_ref[k, :, faces:] = low


def one_hot(k, r, rows, partner_count, info_ref):
    column = info_ref[partner_count, pl.ds(r, rows), k : k + 1]
    return one_where(iota((rows, info_ref.shape[1]), 1).astype(jnp.float32) == column)


def gather(hot, mapped):
    faces = mapped.shape[1] // 2
    parts = product(hot, mapped)
    return parts[:, :faces] + parts[:, faces:]


def in_turn(tiles, ahead, first, then):
    made = {at: first(*tiles[at]) for at in range(min(ahead, len(tiles)))}
    for at, tile in enumerate(tiles):
        if at + ahead < len(tiles):
            made[at + ahead] = first(*tiles[at + ahead])
        then(*tile, made.pop(at))


def slope_kernel(rep_count, slab, packed_ref, mortar_ref, info_ref, state_ref, maps_ref, mapped_ref, labels_ref, arrived):
    planes, total, faces = info_ref.shape
    partner_count = planes - 2
    devices = packed_ref.shape[0]
    blocks = slab * rep_count
    taken = ROWS // rep_count
    copy = pltpu.make_async_copy(
        mortar_ref, info_ref.at[partner_count + 1, pl.ds(0, partner_count * faces)], arrived
    )
    copy.start()
    for device in range(devices):
        state_ref[device * slab : (device + 1) * slab, :] = packed_ref[device, 0:slab, :]
    labels_ref[...] = jnp.zeros_like(labels_ref)
    for vol in range(devices // rep_count):
        for rep in range(rep_count):
            row = rep * taken
            labels_ref[row : row + taken, :] = packed_ref[vol * rep_count + rep, slab : slab + taken, :]
        info_ref[partner_count, vol * blocks : (vol + 1) * blocks, :] = labels_ref[...].T[:blocks]
    owner_column = info_ref[partner_count, :, partner_count : partner_count + 1]
    owners = jnp.broadcast_to(owner_column, (total, faces))
    small_owners = owners.astype(jnp.bfloat16)
    copy.wait()
    map_parts(state_ref[...], partner_count, faces, info_ref, maps_ref, mapped_ref)
    rows = total // 2

    def first(k, r):
        hot = one_hot(k, r, rows, partner_count, info_ref)
        return gather(hot, mapped_ref[k]), product(hot, small_owners)

    def then(k, r, made):
        gathered, partner_owner = made
        span = pl.ds(r, rows)
        agree = partner_owner == info_ref[partner_count, span, partner_count : partner_count + 1]
        small = jnp.exp(-sharpness * jnp.abs(state_ref[span, :] - gathered))
        slope = sharpness * small / ((1.0 + small) * (1.0 + small))
        info_ref[k, span, :] = jnp.where(agree, slope, 0.0)

    tiles = [(k, r) for k in range(partner_count) for r in range(0, total, rows)]
    in_turn(tiles, 2, first, then)


def contact_kernel(order, turns, places_ref, stiffness_ref, info_ref, *refs):
    swaps = len(order)
    pieces, refs = dict(zip(turns, refs[:swaps])), refs[swaps:]
    out_ref, move_ref, stiff_ref, maps_ref, turned_maps_ref, mapped_ref, back_ref, tangent_ref, rows_ref = refs
    total, faces = tangent_ref.shape
    partner_count = info_ref.shape[0] - 2
    blocks = total // swaps
    half = blocks // 2
    rows = total // 2
    for at, d in enumerate(order):
        start = pl.multiple_of((places_ref[0] ^ d) * blocks, ROWS)
        move_ref[pl.ds(start, blocks), :] = pieces[d][...]
        for side in range(2):
            first = pl.multiple_of(start + (places_ref[1] % 2 ^ side) * half, ROWS)
            stiff_ref[pl.ds(first, half), :] = stiffness_ref[side, at]
    map_parts(move_ref[...], partner_count, faces, info_ref, maps_ref, mapped_ref)
    for k in range(partner_count):
        mortar = info_ref[partner_count + 1, k * faces : (k + 1) * faces, :]
        for at, part in enumerate(three_parts(mortar.T)):
            turned_maps_ref[k, at * faces : (at + 1) * faces, :] = part
    for t in range(0, total, LANES):
        rows_ref[:, t : t + LANES] = info_ref[partner_count, t : t + LANES, :].T[:ROWS]
    waiting = []

    def send_back(k, r, parts):
        high, low = halves(product(parts, turned_maps_ref[k]))
        back_ref[k, pl.ds(r, rows), :faces] = high
        back_ref[k, pl.ds(r, rows), faces:] = low

    def then(k, r, gathered):
        span = pl.ds(r, rows)
        traction = stiff_ref[span, :] * info_ref[k, span, :] * (move_ref[span, :] - gathered)
        if k == 0:
            tangent_ref[span, :] = traction
        else:
            tangent_ref[span, :] += traction
        high, low = halves(traction)
        if waiting:
            send_back(*waiting.pop())
        waiting.append((k, r, jnp.concatenate([high, low, high], axis=1)))

    tiles = [(k, r) for k in range(partner_count) for r in range(0, total, rows)]
    in_turn(tiles, 2, lambda k, r: gather(one_hot(k, r, rows, partner_count, info_ref), mapped_ref[k]), then)
    send_back(*waiting.pop())

    def turned(k, r):
        return one_where((iota((rows, total), 0) + r).astype(jnp.float32) == rows_ref[k : k + 1, :])

    for r in range(0, total, rows):
        span = pl.ds(r, rows)
        back = product(turned(0, r), back_ref[0])
        for k in range(1, partner_count):
            back += product(turned(k, r), back_ref[k])
        tangent_ref[span, :] = tangent_ref[span, :] - back[:, :faces] - back[:, faces:]
    devices, slab, _ = out_ref.shape
    for device in range(devices):
        out_ref[device] = tangent_ref[device * slab : (device + 1) * slab, :]


def spread_local(surface_state, direction, stiffness, partners, contact_owner, projection, mortar):
    vol_count, rep_count = lax.axis_size("vol"), lax.axis_size("rep")
    devices = vol_count * rep_count
    vol_index, rep_index = lax.axis_index("vol"), lax.axis_index("rep")
    blocks, share, faces = surface_state.shape
    channels = projection.shape[0]
    partner_count = partners.shape[1]
    slab = blocks // rep_count
    total = blocks * vol_count
    size = channels * ROWS
    vmem = pl.BlockSpec(memory_space=pltpu.VMEM)
    smem = pl.BlockSpec(memory_space=pltpu.SMEM)
    params = pltpu.CompilerParams(vmem_limit_bytes=18 * 1024 * 1024)
    places = jnp.stack([vol_index, rep_index]).astype(jnp.int32)

    def array(*shape, dtype=jnp.float32):
        return jax.ShapeDtypeStruct(shape, dtype)

    def scratch(*shape, dtype=jnp.float32):
        return pltpu.VMEM(shape, dtype)

    def swap(value, axis, d):
        count = lax.axis_size(axis)
        return lax.ppermute(value, axis, [(i, i ^ d) for i in range(count)])

    def exchange(pieces):
        return pieces[:1] + [swap(pieces[d], "rep", d) for d in range(1, rep_count)]

    state = exchange([
        lax.dynamic_slice_in_dim(surface_state, (rep_index ^ d) * slab, slab, 0).reshape(slab * share, faces)
        for d in range(rep_count)
    ])


    move = {0: direction.reshape(blocks * share, faces)}
    step = rep_count // 2
    while step:
        move.update({d ^ step: swap(value, "rep", step) for d, value in move.items()})
        step //= 2

    half = blocks // 2
    stiffness = lax.dynamic_slice_in_dim(stiffness, rep_index % 2 * half, half, 0)
    stiffness = jnp.stack([stiffness, swap(stiffness, "vol", 1)])
    far = list(range(vol_count - 2, 0, -2))
    order = [d ^ near for d in [0] + far for near in range(2)]
    stiffness, state[0] = lax.optimization_barrier((stiffness, state[0]))
    stiffness = [stiffness] + [swap(stiffness, "vol", d) for d in far]

    taken = ROWS // rep_count
    labels = jnp.concatenate([partners.T, contact_owner[None, :]], axis=0).astype(jnp.float32)
    labels = jnp.pad(labels, ((0, ROWS - partner_count - 1), (0, faces - blocks)))
    table = jnp.concatenate([labels, jnp.pad(projection, ((0, 0), (0, faces - channels)))], axis=0)
    state_mix = pl.pallas_call(
        functools.partial(state_mixer_kernel, rep_count, share),
        out_shape=array(2, size, size, dtype=jnp.bfloat16),
        in_specs=[smem, vmem],
        out_specs=vmem,
        compiler_params=params,
    )(places, table)

    sent = pl.pallas_call(
        functools.partial(project_state_kernel, share, slab),
        out_shape=array(channels, slab + taken, faces),
        in_specs=[smem] + [vmem] * (2 + rep_count),
        out_specs=vmem,
        compiler_params=params,
    )(places, state_mix, table, *state)
    sent, stiffness = lax.optimization_barrier((sent, stiffness))
    packed = lax.all_to_all(sent, ("vol", "rep"), 0, 0, tiled=True)

    stiffness = jnp.concatenate(stiffness, axis=0)
    stiffness = jnp.stack([stiffness, swap(stiffness, "rep", 1)])
    move, stiffness = lax.optimization_barrier((move, stiffness))
    moved = list(pl.pallas_call(
        functools.partial(project_move_kernel, rep_count, share),
        out_shape=(array(blocks, faces),) * vol_count,
        in_specs=[smem] + [vmem] * (1 + rep_count),
        out_specs=(vmem,) * vol_count,
        compiler_params=params,
    )(places, projection, *[move[d] for d in range(rep_count)]))
    moved = [swap(piece, "vol", d) if d else piece for d, piece in enumerate(moved)]

    info = pl.pallas_call(
        functools.partial(slope_kernel, rep_count, slab),
        out_shape=array(partner_count + 2, total, faces),
        in_specs=[vmem, pl.BlockSpec(memory_space=pl.ANY)],
        out_specs=vmem,
        scratch_shapes=[
            scratch(total, faces),
            scratch(3 * faces, partner_count * faces, dtype=jnp.bfloat16),
            scratch(partner_count, total, 2 * faces, dtype=jnp.bfloat16),
            scratch(LANES, LANES),
            pltpu.SemaphoreType.DMA,
        ],
        compiler_params=params,
    )(packed, mortar.reshape(partner_count * faces, faces))

    turns = list(range(vol_count))
    turns.insert(vol_count // 2 + 1, turns.pop(vol_count // 2 - 1))
    summed = pl.pallas_call(
        functools.partial(contact_kernel, tuple(order), tuple(turns)),
        out_shape=array(devices, slab, faces),
        in_specs=[smem] + [vmem] * (2 + vol_count),
        out_specs=vmem,
        scratch_shapes=[
            scratch(total, faces),
            scratch(total, faces),
            scratch(3 * faces, partner_count * faces, dtype=jnp.bfloat16),
            scratch(partner_count, 3 * faces, faces, dtype=jnp.bfloat16),
            scratch(partner_count, total, 2 * faces, dtype=jnp.bfloat16),
            scratch(partner_count, total, 2 * faces, dtype=jnp.bfloat16),
            scratch(total, faces),
            scratch(ROWS, total),
        ],
        compiler_params=params,
    )(places, stiffness, info, *[moved[d] for d in turns])
    summed, after = lax.optimization_barrier((summed, places))
    back_mix = pl.pallas_call(
        functools.partial(back_mixer_kernel, rep_count, share),
        out_shape=array(2, size, size, dtype=jnp.bfloat16),
        in_specs=[smem, vmem, smem],
        out_specs=vmem,
        compiler_params=params,
    )(places, projection, after)
    returned = lax.all_to_all(summed, ("vol", "rep"), 0, 0, tiled=True)

    pieces = pl.pallas_call(
        functools.partial(back_kernel, rep_count, share),
        out_shape=array(rep_count, slab * share, faces),
        in_specs=[vmem, vmem],
        out_specs=vmem,
        compiler_params=params,
    )(back_mix, returned)
    pieces = exchange([pieces[d] for d in range(rep_count)])
    out = jnp.zeros((blocks * share, faces), jnp.float32)
    for d in range(rep_count):
        out = lax.dynamic_update_slice_in_dim(out, pieces[d], (rep_index ^ d) * slab * share, 0)
    return out.reshape(blocks, share, faces)


def routed_local(surface_state, direction, stiffness, partners, contact_owner, projection, mortar):
    highest = lax.Precision.HIGHEST
    vol_count = lax.axis_size("vol")
    rep_index = lax.axis_index("rep")
    vol_index = lax.axis_index("vol")
    blocks, channel_share, face_count = surface_state.shape
    partner_count = partners.shape[1]
    capacity = max(2, (2 * blocks + vol_count - 1) // vol_count)
    slot_count = vol_count * capacity
    my_columns = lax.dynamic_slice_in_dim(projection, rep_index * channel_share, channel_share, 1)
    my_rows = lax.dynamic_slice_in_dim(projection, rep_index * channel_share, channel_share, 0)

    def fold_one(piece):
        return jnp.einsum("ij,bjf->bif", my_rows, piece, precision=highest)

    counter = jnp.arange(blocks, dtype=jnp.int32)
    same_owner = contact_owner[:, None] == contact_owner[None, :]
    earlier = counter[:, None] < counter[None, :]
    bucket_rank = jnp.sum((same_owner & earlier).astype(jnp.int32), axis=0)
    slot_of = contact_owner * capacity + bucket_rank
    slot_iota = jnp.arange(slot_count, dtype=jnp.int32)
    matches = slot_iota[:, None] == slot_of[None, :]
    occupied = jnp.any(matches, axis=1).astype(jnp.float32)
    source_row = jnp.sum(jnp.where(matches, counter[None, :], 0), axis=1)
    global_ids = vol_index * blocks + counter
    labels = jnp.concatenate([(global_ids + 1)[:, None], partners], axis=1).astype(jnp.float32)
    send_stiff = (stiffness[source_row] * occupied[:, None]).reshape(
        vol_count, capacity, face_count
    )
    send_labels = (labels[source_row] * occupied[:, None]).reshape(
        vol_count, capacity, partner_count + 1
    )

    def pack(values):
        return (values[source_row] * occupied[:, None, None]).reshape(
            vol_count, capacity, channel_share, face_count
        )

    projected = fold_one(lax.all_gather(surface_state, "rep", axis=1, tiled=True))
    moving = fold_one(lax.all_gather(direction, "rep", axis=1, tiled=True))
    received = (
        lax.all_to_all(pack(projected), "vol", split_axis=0, concat_axis=0, tiled=True),
        lax.all_to_all(pack(moving), "vol", split_axis=0, concat_axis=0, tiled=True),
        lax.all_to_all(send_stiff, "vol", split_axis=0, concat_axis=0, tiled=True),
        lax.all_to_all(send_labels, "vol", split_axis=0, concat_axis=0, tiled=True),
    )
    got_state = received[0].reshape(slot_count, channel_share, face_count)
    got_move = received[1].reshape(slot_count, channel_share, face_count)
    got_stiff = received[2].reshape(slot_count, face_count)
    got_labels = received[3].reshape(slot_count, partner_count + 1).astype(jnp.int32)
    slot_ids = got_labels[:, 0] - 1
    partner_ids = got_labels[:, 1:]
    partner_source = partner_ids // blocks
    candidates = slot_ids.reshape(vol_count, capacity)[partner_source]
    offsets = jnp.arange(capacity, dtype=jnp.int32)
    matched = candidates == partner_ids[..., None]
    found = jnp.any(matched, axis=2).astype(jnp.float32)
    partner_offset = jnp.sum(jnp.where(matched, offsets, 0), axis=2)
    partner_slot = partner_source * capacity + partner_offset
    mapped_state = jnp.einsum("rcf,kfg->krcg", got_state, mortar, precision=highest)
    weights = []
    for column in range(partner_count):
        target = partner_slot[:, column]
        contact_gap = got_state - mapped_state[column][target]
        squashed = jax.nn.sigmoid(sharpness * contact_gap)
        weights.append(
            found[:, column][:, None, None]
            * got_stiff[:, None, :]
            * sharpness
            * squashed
            * (1.0 - squashed)
        )
    partner_slot, weights = (partner_slot, weights)
    mapped_move = jnp.einsum("rcf,kfg->krcg", got_move, mortar, precision=highest)
    tangent = jnp.zeros_like(got_move)
    returns = []
    for column in range(partner_count):
        target = partner_slot[:, column]
        traction = weights[column] * (got_move - mapped_move[column][target])
        tangent = tangent + traction
        returns.append(jax.ops.segment_sum(traction, target, num_segments=slot_count))
    returned = jnp.einsum("krcg,kfg->rcf", jnp.stack(returns), mortar, precision=highest)
    summed = (tangent - returned).reshape(vol_count, capacity, channel_share, face_count)
    returned_tiles = lax.all_to_all(summed, "vol", split_axis=0, concat_axis=0, tiled=True)
    own_tangent = returned_tiles.reshape(slot_count, channel_share, face_count)[slot_of]
    return jnp.einsum(
        "ji,bjf->bif",
        my_columns,
        lax.all_gather(own_tangent, "rep", axis=1, tiled=True),
        precision=highest,
    )


def one_channel_each(mesh, state_shape, partner_shape):
    vol_count, rep_count = mesh.shape["vol"], mesh.shape["rep"]
    total, channels, faces = state_shape
    blocks = total // vol_count
    powers = all(n & (n - 1) == 0 for n in (vol_count, rep_count))
    return (
        powers
        and channels == vol_count * rep_count
        and channels // rep_count == ROWS
        and faces == LANES
        and blocks <= faces
        and blocks % (ROWS // 2 * rep_count) == 0
        and blocks % (2 * ROWS) == 0
        and ROWS % rep_count == 0
        and blocks // rep_count >= ROWS
        and min(vol_count, rep_count) > 1
        and total % LANES == 0
        and partner_shape[1] < ROWS
        and partner_shape[1] * LANES <= total
    )


def solution(mesh):
    placed = (
        P("vol", "rep", None),
        P("vol", "rep", None),
        P("vol", None),
        P("vol", None),
        P("vol"),
        P(),
        P(),
    )

    def program(surface_state, direction, stiffness, partners, *rest):
        fits = one_channel_each(mesh, surface_state.shape, partners.shape)
        plan = spread_local if fits else routed_local
        return jax.shard_map(
            plan, mesh=mesh, in_specs=placed, out_specs=P("vol", "rep", None), check_vma=False
        )(surface_state, direction, stiffness, partners, *rest)

    return program
```

```python
import functools

import jax
import jax.numpy as jnp
from jax import lax
from jax.experimental import pallas as pl
from jax.experimental.pallas import tpu as pltpu
from jax.sharding import PartitionSpec as P

sharpness = 1.5
LANES = 128
ROWS = 8


def halves(value):
    high = value.astype(jnp.bfloat16)
    low = (value - high.astype(jnp.float32)).astype(jnp.bfloat16)
    return high, low


def thirds(value):
    high = value.astype(jnp.bfloat16)
    rest = value - high.astype(jnp.float32)
    middle = rest.astype(jnp.bfloat16)
    return high, middle, (rest - middle.astype(jnp.float32)).astype(jnp.bfloat16)


def product(a, b):
    return jnp.dot(a, b, preferred_element_type=jnp.float32)


def product3(a, b):
    return product(a[0], b[0]) + product(a[1], b[0]) + product(a[0], b[1])


def product6(a, b):
    small = product(a[2], b[0]) + product(a[0], b[2]) + product(a[1], b[1])
    return small + product(a[1], b[0]) + product(a[0], b[1]) + product(a[0], b[0])


def three_parts(value):
    high, low = halves(value)
    return high, high, low


def iota(shape, dim):
    return lax.broadcasted_iota(jnp.int32, shape, dim)


def one_where(cond):
    return jnp.where(cond, 1.0, 0.0).astype(jnp.bfloat16)


def starts(slab):
    return [min(b, slab - ROWS) for b in range(0, slab, ROWS)]


def mixer(projection, channel_of, height, rep_index, rep_count, share, group, split=halves):
    channels = projection.shape[0]
    width = rep_count * group * share
    place = iota((height, channels), 0) // group
    spread = one_where(channel_of(place) == iota((height, channels), 1))
    col = iota((channels, width), 1)
    j = (rep_index ^ (col // (group * share))) * share + col % share
    pick = one_where(iota((channels, width), 0) == j)
    keep = iota((height, width), 0) % group == (iota((height, width), 1) // share) % group
    out = []
    for part in split(projection):
        wide = product(product(spread, part).astype(jnp.bfloat16), pick)
        out.append(jnp.where(keep, wide, 0.0).astype(jnp.bfloat16))
    return out


def back_mixer_kernel(rep_count, share, places_ref, projection_ref, after_ref, mix_ref):
    projection, rep_index = projection_ref[...], places_ref[1]
    parts = mixer(projection, lambda i: i, mix_ref.shape[2], rep_index, rep_count, share, ROWS)
    for at, part in enumerate(parts):
        mix_ref[at] = part.astype(jnp.float32).T.astype(jnp.bfloat16)


def state_mixer_kernel(rep_count, share, places_ref, table_ref, mix_ref):
    channels = table_ref.shape[0] - ROWS
    projection = table_ref[ROWS:, 0:channels]
    parts = mixer(projection, lambda i: i, mix_ref.shape[1], places_ref[1], rep_count, share, ROWS, thirds)
    for at, part in enumerate(parts):
        mix_ref[at] = part


def project_state_kernel(share, slab, places_ref, mix_ref, table_ref, *refs):
    slab_refs, out_ref = refs[:-1], refs[-1]
    channels, length, faces = out_ref.shape
    mix = mix_ref[0], mix_ref[1], mix_ref[2]
    for b in starts(slab):
        pieces = [ref[pl.ds(b * share, ROWS * share), :] for ref in slab_refs]
        out = product6(mix, thirds(jnp.concatenate(pieces, axis=0))).reshape(channels, ROWS, faces)
        out_ref[:, pl.ds(b, ROWS), :] = out
    tail = table_ref[pl.ds(places_ref[1] * (length - slab), length - slab), :]
    out_ref[:, slab:length, :] = jnp.broadcast_to(tail[None], (channels,) + tail.shape)


def project_move_kernel(rep_count, share, places_ref, projection_ref, *refs):
    in_refs, out_refs = refs[:rep_count], refs[rep_count:]
    blocks, faces = out_refs[0].shape
    per = ROWS * share
    me, rep_index = places_ref[0], places_ref[1]

    def channel_of(d):
        return (me ^ d) * rep_count + rep_index

    mix = mixer(projection_ref[...], channel_of, len(out_refs) * ROWS, rep_index, rep_count, share, ROWS)
    groups = blocks // ROWS
    for g in range(0, groups, 2):
        pair = range(g, min(g + 2, groups))
        wide = [jnp.concatenate([ref[pl.ds(p * per, per), :] for ref in in_refs], axis=0) for p in pair]
        out = product3(mix, halves(jnp.concatenate(wide, axis=1)))
        for at, p in enumerate(pair):
            for d, out_ref in enumerate(out_refs):
                out_ref[pl.ds(p * ROWS, ROWS), :] = out[d * ROWS : (d + 1) * ROWS, at * faces : (at + 1) * faces]


def back_kernel(rep_count, share, mix_ref, summed_ref, out_ref):
    channels, slab, faces = summed_ref.shape
    mix = mix_ref[0], mix_ref[1]
    for b in starts(slab):
        values = halves(summed_ref[:, pl.ds(b, ROWS), :].reshape(channels * ROWS, faces))
        out = product3(mix, values).reshape(rep_count, ROWS * share, faces)
        out_ref[:, pl.ds(b * share, ROWS * share), :] = out


def map_parts(values, partner_count, faces, info_ref, maps_ref, mapped_ref):
    for k in range(partner_count):
        mortar = info_ref[partner_count + 1, k * faces : (k + 1) * faces, :]
        for at, part in enumerate(three_parts(mortar)):
            maps_ref[at * faces : (at + 1) * faces, k * faces : (k + 1) * faces] = part
    high, low = halves(values)
    mapped = product(jnp.concatenate([high, low, high], axis=1), maps_ref[...])
    for k in range(partner_count):
        high, low = halves(mapped[:, k * faces : (k + 1) * faces])
        mapped_ref[k, :, :faces] = high
        mapped_ref[k, :, faces:] = low


def one_hot(k, r, rows, partner_count, info_ref):
    column = info_ref[partner_count, pl.ds(r, rows), k : k + 1]
    return one_where(iota((rows, info_ref.shape[1]), 1).astype(jnp.float32) == column)


def gather(hot, mapped):
    faces = mapped.shape[1] // 2
    parts = product(hot, mapped)
    return parts[:, :faces] + parts[:, faces:]


def in_turn(tiles, ahead, first, then):
    made = {at: first(*tiles[at]) for at in range(min(ahead, len(tiles)))}
    for at, tile in enumerate(tiles):
        if at + ahead < len(tiles):
            made[at + ahead] = first(*tiles[at + ahead])
        then(*tile, made.pop(at))


def slope_kernel(rep_count, slab, packed_ref, mortar_ref, info_ref, state_ref, maps_ref, mapped_ref, extra_ref, labels_ref, arrived):
    planes, total, faces = info_ref.shape
    partner_count = planes - 2
    devices = packed_ref.shape[0]
    blocks = slab * rep_count
    taken = ROWS // rep_count
    copy = pltpu.make_async_copy(
        mortar_ref, info_ref.at[partner_count + 1, pl.ds(0, partner_count * faces)], arrived
    )
    copy.start()
    for device in range(devices):
        state_ref[device * slab : (device + 1) * slab, :] = packed_ref[device, 0:slab, :]
    labels_ref[...] = jnp.zeros_like(labels_ref)
    for vol in range(devices // rep_count):
        for rep in range(rep_count):
            row = rep * taken
            labels_ref[row : row + taken, :] = packed_ref[vol * rep_count + rep, slab : slab + taken, :]
        info_ref[partner_count, vol * blocks : (vol + 1) * blocks, :] = labels_ref[...].T[:blocks]
    owner_column = info_ref[partner_count, :, partner_count : partner_count + 1]
    owners = jnp.broadcast_to(owner_column, (total, faces))
    small_owners = owners.astype(jnp.bfloat16)
    copy.wait()
    for k in range(partner_count):
        high, middle, low = thirds(info_ref[partner_count + 1, k * faces : (k + 1) * faces, :])
        for at, part in enumerate((high, high, middle, high, low, middle)):
            maps_ref[at * faces : (at + 1) * faces, k * faces : (k + 1) * faces] = part
    high, middle, low = thirds(state_ref[...])
    mapped = product(jnp.concatenate([high, middle, high, low, high, middle], axis=1), maps_ref[...])
    for k in range(partner_count):
        high, middle, low = thirds(mapped[:, k * faces : (k + 1) * faces])
        mapped_ref[k, :, :faces] = high
        mapped_ref[k, :, faces:] = middle
        extra_ref[k, :, :faces] = low
        extra_ref[k, :, faces:] = small_owners
    rows = total // 2

    def first(k, r):
        hot = one_hot(k, r, rows, partner_count, info_ref)
        return gather(hot, mapped_ref[k]), product(hot, extra_ref[k])

    def then(k, r, made):
        gathered, extra = made
        gathered = gathered + extra[:, :faces]
        span = pl.ds(r, rows)
        agree = extra[:, faces:] == info_ref[partner_count, span, partner_count : partner_count + 1]
        small = jnp.exp(-sharpness * jnp.abs(state_ref[span, :] - gathered))
        slope = sharpness * small / ((1.0 + small) * (1.0 + small))
        info_ref[k, span, :] = jnp.where(agree, slope, 0.0)

    tiles = [(k, r) for k in range(partner_count) for r in range(0, total, rows)]
    in_turn(tiles, 2, first, then)


def contact_kernel(order, turns, places_ref, stiffness_ref, info_ref, *refs):
    swaps = len(order)
    pieces, refs = dict(zip(turns, refs[:swaps])), refs[swaps:]
    out_ref, move_ref, stiff_ref, maps_ref, turned_maps_ref, mapped_ref, back_ref, tangent_ref, rows_ref = refs
    total, faces = tangent_ref.shape
    partner_count = info_ref.shape[0] - 2
    blocks = total // swaps
    half = blocks // 2
    rows = total // 2
    for at, d in enumerate(order):
        start = pl.multiple_of((places_ref[0] ^ d) * blocks, ROWS)
        move_ref[pl.ds(start, blocks), :] = pieces[d][...]
        for side in range(2):
            first = pl.multiple_of(start + (places_ref[1] % 2 ^ side) * half, ROWS)
            stiff_ref[pl.ds(first, half), :] = stiffness_ref[side, at]
    map_parts(move_ref[...], partner_count, faces, info_ref, maps_ref, mapped_ref)
    for k in range(partner_count):
        mortar = info_ref[partner_count + 1, k * faces : (k + 1) * faces, :]
        for at, part in enumerate(three_parts(mortar.T)):
            turned_maps_ref[k, at * faces : (at + 1) * faces, :] = part
    for t in range(0, total, LANES):
        rows_ref[:, t : t + LANES] = info_ref[partner_count, t : t + LANES, :].T[:ROWS]
    waiting = []

    def send_back(k, r, parts):
        high, low = halves(product(parts, turned_maps_ref[k]))
        back_ref[k, pl.ds(r, rows), :faces] = high
        back_ref[k, pl.ds(r, rows), faces:] = low

    def then(k, r, gathered):
        span = pl.ds(r, rows)
        traction = stiff_ref[span, :] * info_ref[k, span, :] * (move_ref[span, :] - gathered)
        if k == 0:
            tangent_ref[span, :] = traction
        else:
            tangent_ref[span, :] += traction
        high, low = halves(traction)
        if waiting:
            send_back(*waiting.pop())
        waiting.append((k, r, jnp.concatenate([high, low, high], axis=1)))

    tiles = [(k, r) for k in range(partner_count) for r in range(0, total, rows)]
    in_turn(tiles, 2, lambda k, r: gather(one_hot(k, r, rows, partner_count, info_ref), mapped_ref[k]), then)
    send_back(*waiting.pop())

    def turned(k, r):
        return one_where((iota((rows, total), 0) + r).astype(jnp.float32) == rows_ref[k : k + 1, :])

    for r in range(0, total, rows):
        span = pl.ds(r, rows)
        back = product(turned(0, r), back_ref[0])
        for k in range(1, partner_count):
            back += product(turned(k, r), back_ref[k])
        tangent_ref[span, :] = tangent_ref[span, :] - back[:, :faces] - back[:, faces:]
    devices, slab, _ = out_ref.shape
    for device in range(devices):
        out_ref[device] = tangent_ref[device * slab : (device + 1) * slab, :]


def spread_local(surface_state, direction, stiffness, partners, contact_owner, projection, mortar):
    vol_count, rep_count = lax.axis_size("vol"), lax.axis_size("rep")
    devices = vol_count * rep_count
    vol_index, rep_index = lax.axis_index("vol"), lax.axis_index("rep")
    blocks, share, faces = surface_state.shape
    channels = projection.shape[0]
    partner_count = partners.shape[1]
    slab = blocks // rep_count
    total = blocks * vol_count
    size = channels * ROWS
    vmem = pl.BlockSpec(memory_space=pltpu.VMEM)
    smem = pl.BlockSpec(memory_space=pltpu.SMEM)
    params = pltpu.CompilerParams(vmem_limit_bytes=18 * 1024 * 1024)
    places = jnp.stack([vol_index, rep_index]).astype(jnp.int32)

    def array(*shape, dtype=jnp.float32):
        return jax.ShapeDtypeStruct(shape, dtype)

    def scratch(*shape, dtype=jnp.float32):
        return pltpu.VMEM(shape, dtype)

    def swap(value, axis, d):
        count = lax.axis_size(axis)
        return lax.ppermute(value, axis, [(i, i ^ d) for i in range(count)])

    def exchange(pieces):
        return pieces[:1] + [swap(pieces[d], "rep", d) for d in range(1, rep_count)]

    state = exchange([
        lax.dynamic_slice_in_dim(surface_state, (rep_index ^ d) * slab, slab, 0).reshape(slab * share, faces)
        for d in range(rep_count)
    ])


    move = {0: direction.reshape(blocks * share, faces)}
    step = rep_count // 2
    while step:
        move.update({d ^ step: swap(value, "rep", step) for d, value in move.items()})
        step //= 2

    half = blocks // 2
    stiffness = lax.dynamic_slice_in_dim(stiffness, rep_index % 2 * half, half, 0)
    stiffness = jnp.stack([stiffness, swap(stiffness, "vol", 1)])
    far = list(range(vol_count - 2, 0, -2))
    order = [d ^ near for d in [0] + far for near in range(2)]
    stiffness, state[0] = lax.optimization_barrier((stiffness, state[0]))
    stiffness = [stiffness] + [swap(stiffness, "vol", d) for d in far]

    taken = ROWS // rep_count
    labels = jnp.concatenate([partners.T, contact_owner[None, :]], axis=0).astype(jnp.float32)
    labels = jnp.pad(labels, ((0, ROWS - partner_count - 1), (0, faces - blocks)))
    table = jnp.concatenate([labels, jnp.pad(projection, ((0, 0), (0, faces - channels)))], axis=0)
    state_mix = pl.pallas_call(
        functools.partial(state_mixer_kernel, rep_count, share),
        out_shape=array(3, size, size, dtype=jnp.bfloat16),
        in_specs=[smem, vmem],
        out_specs=vmem,
        compiler_params=params,
    )(places, table)

    sent = pl.pallas_call(
        functools.partial(project_state_kernel, share, slab),
        out_shape=array(channels, slab + taken, faces),
        in_specs=[smem] + [vmem] * (2 + rep_count),
        out_specs=vmem,
        compiler_params=params,
    )(places, state_mix, table, *state)
    sent, stiffness = lax.optimization_barrier((sent, stiffness))
    packed = lax.all_to_all(sent, ("vol", "rep"), 0, 0, tiled=True)

    stiffness = jnp.concatenate(stiffness, axis=0)
    stiffness = jnp.stack([stiffness, swap(stiffness, "rep", 1)])
    move, stiffness = lax.optimization_barrier((move, stiffness))
    moved = list(pl.pallas_call(
        functools.partial(project_move_kernel, rep_count, share),
        out_shape=(array(blocks, faces),) * vol_count,
        in_specs=[smem] + [vmem] * (1 + rep_count),
        out_specs=(vmem,) * vol_count,
        compiler_params=params,
    )(places, projection, *[move[d] for d in range(rep_count)]))
    moved = [swap(piece, "vol", d) if d else piece for d, piece in enumerate(moved)]

    info = pl.pallas_call(
        functools.partial(slope_kernel, rep_count, slab),
        out_shape=array(partner_count + 2, total, faces),
        in_specs=[vmem, pl.BlockSpec(memory_space=pl.ANY)],
        out_specs=vmem,
        scratch_shapes=[
            scratch(total, faces),
            scratch(6 * faces, partner_count * faces, dtype=jnp.bfloat16),
            scratch(partner_count, total, 2 * faces, dtype=jnp.bfloat16),
            scratch(partner_count, total, 2 * faces, dtype=jnp.bfloat16),
            scratch(LANES, LANES),
            pltpu.SemaphoreType.DMA,
        ],
        compiler_params=params,
    )(packed, mortar.reshape(partner_count * faces, faces))

    turns = list(range(vol_count))
    turns.insert(vol_count // 2 + 1, turns.pop(vol_count // 2 - 1))
    summed = pl.pallas_call(
        functools.partial(contact_kernel, tuple(order), tuple(turns)),
        out_shape=array(devices, slab, faces),
        in_specs=[smem] + [vmem] * (2 + vol_count),
        out_specs=vmem,
        scratch_shapes=[
            scratch(total, faces),
            scratch(total, faces),
            scratch(3 * faces, partner_count * faces, dtype=jnp.bfloat16),
            scratch(partner_count, 3 * faces, faces, dtype=jnp.bfloat16),
            scratch(partner_count, total, 2 * faces, dtype=jnp.bfloat16),
            scratch(partner_count, total, 2 * faces, dtype=jnp.bfloat16),
            scratch(total, faces),
            scratch(ROWS, total),
        ],
        compiler_params=params,
    )(places, stiffness, info, *[moved[d] for d in turns])
    summed, after = lax.optimization_barrier((summed, places))
    back_mix = pl.pallas_call(
        functools.partial(back_mixer_kernel, rep_count, share),
        out_shape=array(2, size, size, dtype=jnp.bfloat16),
        in_specs=[smem, vmem, smem],
        out_specs=vmem,
        compiler_params=params,
    )(places, projection, after)
    returned = lax.all_to_all(summed, ("vol", "rep"), 0, 0, tiled=True)

    pieces = pl.pallas_call(
        functools.partial(back_kernel, rep_count, share),
        out_shape=array(rep_count, slab * share, faces),
        in_specs=[vmem, vmem],
        out_specs=vmem,
        compiler_params=params,
    )(back_mix, returned)
    pieces = exchange([pieces[d] for d in range(rep_count)])
    out = jnp.zeros((blocks * share, faces), jnp.float32)
    for d in range(rep_count):
        out = lax.dynamic_update_slice_in_dim(out, pieces[d], (rep_index ^ d) * slab * share, 0)
    return out.reshape(blocks, share, faces)


def routed_local(surface_state, direction, stiffness, partners, contact_owner, projection, mortar):
    highest = lax.Precision.HIGHEST
    vol_count = lax.axis_size("vol")
    rep_index = lax.axis_index("rep")
    vol_index = lax.axis_index("vol")
    blocks, channel_share, face_count = surface_state.shape
    partner_count = partners.shape[1]
    capacity = max(2, (2 * blocks + vol_count - 1) // vol_count)
    slot_count = vol_count * capacity
    my_columns = lax.dynamic_slice_in_dim(projection, rep_index * channel_share, channel_share, 1)
    my_rows = lax.dynamic_slice_in_dim(projection, rep_index * channel_share, channel_share, 0)

    def fold_one(piece):
        return jnp.einsum("ij,bjf->bif", my_rows, piece, precision=highest)

    counter = jnp.arange(blocks, dtype=jnp.int32)
    same_owner = contact_owner[:, None] == contact_owner[None, :]
    earlier = counter[:, None] < counter[None, :]
    bucket_rank = jnp.sum((same_owner & earlier).astype(jnp.int32), axis=0)
    slot_of = contact_owner * capacity + bucket_rank
    slot_iota = jnp.arange(slot_count, dtype=jnp.int32)
    matches = slot_iota[:, None] == slot_of[None, :]
    occupied = jnp.any(matches, axis=1).astype(jnp.float32)
    source_row = jnp.sum(jnp.where(matches, counter[None, :], 0), axis=1)
    global_ids = vol_index * blocks + counter
    labels = jnp.concatenate([(global_ids + 1)[:, None], partners], axis=1).astype(jnp.float32)
    send_stiff = (stiffness[source_row] * occupied[:, None]).reshape(
        vol_count, capacity, face_count
    )
    send_labels = (labels[source_row] * occupied[:, None]).reshape(
        vol_count, capacity, partner_count + 1
    )

    def pack(values):
        return (values[source_row] * occupied[:, None, None]).reshape(
            vol_count, capacity, channel_share, face_count
        )

    projected = fold_one(lax.all_gather(surface_state, "rep", axis=1, tiled=True))
    moving = fold_one(lax.all_gather(direction, "rep", axis=1, tiled=True))
    received = (
        lax.all_to_all(pack(projected), "vol", split_axis=0, concat_axis=0, tiled=True),
        lax.all_to_all(pack(moving), "vol", split_axis=0, concat_axis=0, tiled=True),
        lax.all_to_all(send_stiff, "vol", split_axis=0, concat_axis=0, tiled=True),
        lax.all_to_all(send_labels, "vol", split_axis=0, concat_axis=0, tiled=True),
    )
    got_state = received[0].reshape(slot_count, channel_share, face_count)
    got_move = received[1].reshape(slot_count, channel_share, face_count)
    got_stiff = received[2].reshape(slot_count, face_count)
    got_labels = received[3].reshape(slot_count, partner_count + 1).astype(jnp.int32)
    slot_ids = got_labels[:, 0] - 1
    partner_ids = got_labels[:, 1:]
    partner_source = partner_ids // blocks
    candidates = slot_ids.reshape(vol_count, capacity)[partner_source]
    offsets = jnp.arange(capacity, dtype=jnp.int32)
    matched = candidates == partner_ids[..., None]
    found = jnp.any(matched, axis=2).astype(jnp.float32)
    partner_offset = jnp.sum(jnp.where(matched, offsets, 0), axis=2)
    partner_slot = partner_source * capacity + partner_offset
    mapped_state = jnp.einsum("rcf,kfg->krcg", got_state, mortar, precision=highest)
    weights = []
    for column in range(partner_count):
        target = partner_slot[:, column]
        contact_gap = got_state - mapped_state[column][target]
        squashed = jax.nn.sigmoid(sharpness * contact_gap)
        weights.append(
            found[:, column][:, None, None]
            * got_stiff[:, None, :]
            * sharpness
            * squashed
            * (1.0 - squashed)
        )
    partner_slot, weights = (partner_slot, weights)
    mapped_move = jnp.einsum("rcf,kfg->krcg", got_move, mortar, precision=highest)
    tangent = jnp.zeros_like(got_move)
    returns = []
    for column in range(partner_count):
        target = partner_slot[:, column]
        traction = weights[column] * (got_move - mapped_move[column][target])
        tangent = tangent + traction
        returns.append(jax.ops.segment_sum(traction, target, num_segments=slot_count))
    returned = jnp.einsum("krcg,kfg->rcf", jnp.stack(returns), mortar, precision=highest)
    summed = (tangent - returned).reshape(vol_count, capacity, channel_share, face_count)
    returned_tiles = lax.all_to_all(summed, "vol", split_axis=0, concat_axis=0, tiled=True)
    own_tangent = returned_tiles.reshape(slot_count, channel_share, face_count)[slot_of]
    return jnp.einsum(
        "ji,bjf->bif",
        my_columns,
        lax.all_gather(own_tangent, "rep", axis=1, tiled=True),
        precision=highest,
    )


def one_channel_each(mesh, state_shape, partner_shape):
    vol_count, rep_count = mesh.shape["vol"], mesh.shape["rep"]
    total, channels, faces = state_shape
    blocks = total // vol_count
    powers = all(n & (n - 1) == 0 for n in (vol_count, rep_count))
    return (
        powers
        and channels == vol_count * rep_count
        and channels // rep_count == ROWS
        and faces == LANES
        and blocks <= faces
        and blocks % (ROWS // 2 * rep_count) == 0
        and blocks % (2 * ROWS) == 0
        and ROWS % rep_count == 0
        and blocks // rep_count >= ROWS
        and min(vol_count, rep_count) > 1
        and total % LANES == 0
        and partner_shape[1] < ROWS
        and partner_shape[1] * LANES <= total
    )


def solution(mesh):
    placed = (
        P("vol", "rep", None),
        P("vol", "rep", None),
        P("vol", None),
        P("vol", None),
        P("vol"),
        P(),
        P(),
    )

    def program(surface_state, direction, stiffness, partners, *rest):
        fits = one_channel_each(mesh, surface_state.shape, partners.shape)
        plan = spread_local if fits else routed_local
        return jax.shard_map(
            plan, mesh=mesh, in_specs=placed, out_specs=P("vol", "rep", None), check_vma=False
        )(surface_state, direction, stiffness, partners, *rest)

    return program
```

```python
import functools

import jax
import jax.numpy as jnp
from jax import lax
from jax.experimental import pallas as pl
from jax.experimental.pallas import tpu as pltpu
from jax.sharding import PartitionSpec as P

sharpness = 1.5
LANES = 128
ROWS = 8


def halves(value):
    high = value.astype(jnp.bfloat16)
    low = (value - high.astype(jnp.float32)).astype(jnp.bfloat16)
    return high, low


def thirds(value):
    high = value.astype(jnp.bfloat16)
    rest = value - high.astype(jnp.float32)
    middle = rest.astype(jnp.bfloat16)
    return high, middle, (rest - middle.astype(jnp.float32)).astype(jnp.bfloat16)


def product(a, b):
    return jnp.dot(a, b, preferred_element_type=jnp.float32)


def product3(a, b):
    return product(a[0], b[0]) + product(a[1], b[0]) + product(a[0], b[1])


def product6(a, b):
    small = product(a[2], b[0]) + product(a[0], b[2]) + product(a[1], b[1])
    return small + product(a[1], b[0]) + product(a[0], b[1]) + product(a[0], b[0])


def three_parts(value):
    high, low = halves(value)
    return high, high, low


def iota(shape, dim):
    return lax.broadcasted_iota(jnp.int32, shape, dim)


def one_where(cond):
    return jnp.where(cond, 1.0, 0.0).astype(jnp.bfloat16)


def starts(slab):
    return [min(b, slab - ROWS) for b in range(0, slab, ROWS)]


def mixer(projection, channel_of, height, rep_index, rep_count, share, group, split=halves):
    channels = projection.shape[0]
    width = rep_count * group * share
    place = iota((height, channels), 0) // group
    spread = one_where(channel_of(place) == iota((height, channels), 1))
    col = iota((channels, width), 1)
    j = (rep_index ^ (col // (group * share))) * share + col % share
    pick = one_where(iota((channels, width), 0) == j)
    keep = iota((height, width), 0) % group == (iota((height, width), 1) // share) % group
    out = []
    for part in split(projection):
        wide = product(product(spread, part).astype(jnp.bfloat16), pick)
        out.append(jnp.where(keep, wide, 0.0).astype(jnp.bfloat16))
    return out


def back_mixer_kernel(rep_count, share, places_ref, projection_ref, after_ref, mix_ref):
    projection, rep_index = projection_ref[...], places_ref[1]
    parts = mixer(projection, lambda i: i, mix_ref.shape[2], rep_index, rep_count, share, ROWS)
    for at, part in enumerate(parts):
        mix_ref[at] = part.astype(jnp.float32).T.astype(jnp.bfloat16)


def state_mixer_kernel(rep_count, share, places_ref, table_ref, mix_ref):
    channels = table_ref.shape[0] - ROWS
    projection = table_ref[ROWS:, 0:channels]
    parts = mixer(projection, lambda i: i, mix_ref.shape[1], places_ref[1], rep_count, share, ROWS, thirds)
    for at, part in enumerate(parts):
        mix_ref[at] = part


def project_state_kernel(share, slab, places_ref, mix_ref, table_ref, *refs):
    slab_refs, out_ref = refs[:-1], refs[-1]
    channels, length, faces = out_ref.shape
    mix = mix_ref[0], mix_ref[1], mix_ref[2]
    groups = starts(slab)
    for at in range(0, len(groups), 2):
        pair = groups[at : at + 2]
        wide = [
            jnp.concatenate([ref[pl.ds(b * share, ROWS * share), :] for ref in slab_refs], axis=0) for b in pair
        ]
        out = product6(mix, thirds(jnp.concatenate(wide, axis=1)))
        for which, b in enumerate(pair):
            part = out[:, which * faces : (which + 1) * faces]
            out_ref[:, pl.ds(b, ROWS), :] = part.reshape(channels, ROWS, faces)
    tail = table_ref[pl.ds(places_ref[1] * (length - slab), length - slab), :]
    out_ref[:, slab:length, :] = jnp.broadcast_to(tail[None], (channels,) + tail.shape)


def project_move_kernel(rep_count, share, places_ref, projection_ref, *refs):
    in_refs, out_refs = refs[:rep_count], refs[rep_count:]
    blocks, faces = out_refs[0].shape
    per = ROWS * share
    me, rep_index = places_ref[0], places_ref[1]

    def channel_of(d):
        return (me ^ d) * rep_count + rep_index

    mix = mixer(projection_ref[...], channel_of, len(out_refs) * ROWS, rep_index, rep_count, share, ROWS)
    groups = blocks // ROWS
    for g in range(0, groups, 2):
        pair = range(g, min(g + 2, groups))
        wide = [jnp.concatenate([ref[pl.ds(p * per, per), :] for ref in in_refs], axis=0) for p in pair]
        out = product3(mix, halves(jnp.concatenate(wide, axis=1)))
        for at, p in enumerate(pair):
            for d, out_ref in enumerate(out_refs):
                out_ref[pl.ds(p * ROWS, ROWS), :] = out[d * ROWS : (d + 1) * ROWS, at * faces : (at + 1) * faces]


def back_kernel(rep_count, share, mix_ref, summed_ref, out_ref):
    channels, slab, faces = summed_ref.shape
    mix = mix_ref[0], mix_ref[1]
    for b in starts(slab):
        values = halves(summed_ref[:, pl.ds(b, ROWS), :].reshape(channels * ROWS, faces))
        out = product3(mix, values).reshape(rep_count, ROWS * share, faces)
        out_ref[:, pl.ds(b * share, ROWS * share), :] = out


def map_parts(values, partner_count, faces, info_ref, maps_ref, mapped_ref):
    for k in range(partner_count):
        mortar = info_ref[partner_count + 1, k * faces : (k + 1) * faces, :]
        for at, part in enumerate(three_parts(mortar)):
            maps_ref[at * faces : (at + 1) * faces, k * faces : (k + 1) * faces] = part
    high, low = halves(values)
    mapped = product(jnp.concatenate([high, low, high], axis=1), maps_ref[...])
    for k in range(partner_count):
        high, low = halves(mapped[:, k * faces : (k + 1) * faces])
        mapped_ref[k, :, :faces] = high
        mapped_ref[k, :, faces:] = low


def one_hot(k, r, rows, partner_count, info_ref):
    column = info_ref[partner_count, pl.ds(r, rows), k : k + 1]
    return one_where(iota((rows, info_ref.shape[1]), 1).astype(jnp.float32) == column)


def gather(hot, mapped):
    faces = mapped.shape[1] // 2
    parts = product(hot, mapped)
    return parts[:, :faces] + parts[:, faces:]


def in_turn(tiles, ahead, first, then):
    made = {at: first(*tiles[at]) for at in range(min(ahead, len(tiles)))}
    for at, tile in enumerate(tiles):
        if at + ahead < len(tiles):
            made[at + ahead] = first(*tiles[at + ahead])
        then(*tile, made.pop(at))


def slope_kernel(rep_count, slab, packed_ref, mortar_ref, info_ref, state_ref, maps_ref, mapped_ref, extra_ref, labels_ref, arrived):
    planes, total, faces = info_ref.shape
    partner_count = planes - 2
    devices = packed_ref.shape[0]
    blocks = slab * rep_count
    taken = ROWS // rep_count
    copy = pltpu.make_async_copy(
        mortar_ref, info_ref.at[partner_count + 1, pl.ds(0, partner_count * faces)], arrived
    )
    copy.start()
    for device in range(devices):
        state_ref[device * slab : (device + 1) * slab, :] = packed_ref[device, 0:slab, :]
    labels_ref[...] = jnp.zeros_like(labels_ref)
    for vol in range(devices // rep_count):
        for rep in range(rep_count):
            row = rep * taken
            labels_ref[row : row + taken, :] = packed_ref[vol * rep_count + rep, slab : slab + taken, :]
        info_ref[partner_count, vol * blocks : (vol + 1) * blocks, :] = labels_ref[...].T[:blocks]
    owner_column = info_ref[partner_count, :, partner_count : partner_count + 1]
    owners = jnp.broadcast_to(owner_column, (total, faces))
    small_owners = owners.astype(jnp.bfloat16)
    copy.wait()
    for k in range(partner_count):
        high, middle, low = thirds(info_ref[partner_count + 1, k * faces : (k + 1) * faces, :])
        for at, part in enumerate((high, high, middle, high, low, middle)):
            maps_ref[at * faces : (at + 1) * faces, k * faces : (k + 1) * faces] = part
    high, middle, low = thirds(state_ref[...])
    mapped = product(jnp.concatenate([high, middle, high, low, high, middle], axis=1), maps_ref[...])
    for k in range(partner_count):
        high, middle, low = thirds(mapped[:, k * faces : (k + 1) * faces])
        mapped_ref[k, :, :faces] = high
        mapped_ref[k, :, faces:] = middle
        extra_ref[k, :, :faces] = low
        extra_ref[k, :, faces:] = small_owners
    rows = total // 2

    def first(k, r):
        hot = one_hot(k, r, rows, partner_count, info_ref)
        return gather(hot, mapped_ref[k]), product(hot, extra_ref[k])

    def then(k, r, made):
        gathered, extra = made
        gathered = gathered + extra[:, :faces]
        span = pl.ds(r, rows)
        agree = extra[:, faces:] == info_ref[partner_count, span, partner_count : partner_count + 1]
        small = jnp.exp(-sharpness * jnp.abs(state_ref[span, :] - gathered))
        slope = sharpness * small / ((1.0 + small) * (1.0 + small))
        info_ref[k, span, :] = jnp.where(agree, slope, 0.0)

    tiles = [(k, r) for k in range(partner_count) for r in range(0, total, rows)]
    in_turn(tiles, 2, first, then)


def contact_kernel(order, turns, places_ref, stiffness_ref, info_ref, *refs):
    swaps = len(order)
    pieces, refs = dict(zip(turns, refs[:swaps])), refs[swaps:]
    out_ref, move_ref, stiff_ref, maps_ref, turned_maps_ref, mapped_ref, back_ref, tangent_ref, rows_ref = refs
    total, faces = tangent_ref.shape
    partner_count = info_ref.shape[0] - 2
    blocks = total // swaps
    half = blocks // 2
    rows = total // 2
    for at, d in enumerate(order):
        start = pl.multiple_of((places_ref[0] ^ d) * blocks, ROWS)
        move_ref[pl.ds(start, blocks), :] = pieces[d][...]
        for side in range(2):
            first = pl.multiple_of(start + (places_ref[1] % 2 ^ side) * half, ROWS)
            stiff_ref[pl.ds(first, half), :] = stiffness_ref[side, at]
    map_parts(move_ref[...], partner_count, faces, info_ref, maps_ref, mapped_ref)
    for k in range(partner_count):
        mortar = info_ref[partner_count + 1, k * faces : (k + 1) * faces, :]
        for at, part in enumerate(three_parts(mortar.T)):
            turned_maps_ref[k, at * faces : (at + 1) * faces, :] = part
    for t in range(0, total, LANES):
        rows_ref[:, t : t + LANES] = info_ref[partner_count, t : t + LANES, :].T[:ROWS]
    waiting = []

    def send_back(k, r, parts):
        high, low = halves(product(parts, turned_maps_ref[k]))
        back_ref[k, pl.ds(r, rows), :faces] = high
        back_ref[k, pl.ds(r, rows), faces:] = low

    def then(k, r, gathered):
        span = pl.ds(r, rows)
        traction = stiff_ref[span, :] * info_ref[k, span, :] * (move_ref[span, :] - gathered)
        if k == 0:
            tangent_ref[span, :] = traction
        else:
            tangent_ref[span, :] += traction
        high, low = halves(traction)
        if waiting:
            send_back(*waiting.pop())
        waiting.append((k, r, jnp.concatenate([high, low, high], axis=1)))

    tiles = [(k, r) for k in range(partner_count) for r in range(0, total, rows)]
    in_turn(tiles, 2, lambda k, r: gather(one_hot(k, r, rows, partner_count, info_ref), mapped_ref[k]), then)
    send_back(*waiting.pop())

    def turned(k, r):
        return one_where((iota((rows, total), 0) + r).astype(jnp.float32) == rows_ref[k : k + 1, :])

    for r in range(0, total, rows):
        span = pl.ds(r, rows)
        back = product(turned(0, r), back_ref[0])
        for k in range(1, partner_count):
            back += product(turned(k, r), back_ref[k])
        tangent_ref[span, :] = tangent_ref[span, :] - back[:, :faces] - back[:, faces:]
    devices, slab, _ = out_ref.shape
    for device in range(devices):
        out_ref[device] = tangent_ref[device * slab : (device + 1) * slab, :]


def spread_local(surface_state, direction, stiffness, partners, contact_owner, projection, mortar):
    vol_count, rep_count = lax.axis_size("vol"), lax.axis_size("rep")
    devices = vol_count * rep_count
    vol_index, rep_index = lax.axis_index("vol"), lax.axis_index("rep")
    blocks, share, faces = surface_state.shape
    channels = projection.shape[0]
    partner_count = partners.shape[1]
    slab = blocks // rep_count
    total = blocks * vol_count
    size = channels * ROWS
    vmem = pl.BlockSpec(memory_space=pltpu.VMEM)
    smem = pl.BlockSpec(memory_space=pltpu.SMEM)
    params = pltpu.CompilerParams(vmem_limit_bytes=18 * 1024 * 1024)
    places = jnp.stack([vol_index, rep_index]).astype(jnp.int32)

    def array(*shape, dtype=jnp.float32):
        return jax.ShapeDtypeStruct(shape, dtype)

    def scratch(*shape, dtype=jnp.float32):
        return pltpu.VMEM(shape, dtype)

    def swap(value, axis, d):
        count = lax.axis_size(axis)
        return lax.ppermute(value, axis, [(i, i ^ d) for i in range(count)])

    def exchange(pieces):
        return pieces[:1] + [swap(pieces[d], "rep", d) for d in range(1, rep_count)]

    state = exchange([
        lax.dynamic_slice_in_dim(surface_state, (rep_index ^ d) * slab, slab, 0).reshape(slab * share, faces)
        for d in range(rep_count)
    ])


    move = {0: direction.reshape(blocks * share, faces)}
    step = rep_count // 2
    while step:
        move.update({d ^ step: swap(value, "rep", step) for d, value in move.items()})
        step //= 2

    half = blocks // 2
    stiffness = lax.dynamic_slice_in_dim(stiffness, rep_index % 2 * half, half, 0)
    stiffness = jnp.stack([stiffness, swap(stiffness, "vol", 1)])
    far = list(range(vol_count - 2, 0, -2))
    order = [d ^ near for d in [0] + far for near in range(2)]
    stiffness, state[0] = lax.optimization_barrier((stiffness, state[0]))
    stiffness = [stiffness] + [swap(stiffness, "vol", d) for d in far]

    taken = ROWS // rep_count
    labels = jnp.concatenate([partners.T, contact_owner[None, :]], axis=0).astype(jnp.float32)
    labels = jnp.pad(labels, ((0, ROWS - partner_count - 1), (0, faces - blocks)))
    table = jnp.concatenate([labels, jnp.pad(projection, ((0, 0), (0, faces - channels)))], axis=0)
    state_mix = pl.pallas_call(
        functools.partial(state_mixer_kernel, rep_count, share),
        out_shape=array(3, size, size, dtype=jnp.bfloat16),
        in_specs=[smem, vmem],
        out_specs=vmem,
        compiler_params=params,
    )(places, table)

    sent = pl.pallas_call(
        functools.partial(project_state_kernel, share, slab),
        out_shape=array(channels, slab + taken, faces),
        in_specs=[smem] + [vmem] * (2 + rep_count),
        out_specs=vmem,
        compiler_params=params,
    )(places, state_mix, table, *state)
    sent, stiffness = lax.optimization_barrier((sent, stiffness))
    packed = lax.all_to_all(sent, ("vol", "rep"), 0, 0, tiled=True)

    stiffness = jnp.concatenate(stiffness, axis=0)
    stiffness = jnp.stack([stiffness, swap(stiffness, "rep", 1)])
    move, stiffness = lax.optimization_barrier((move, stiffness))
    moved = list(pl.pallas_call(
        functools.partial(project_move_kernel, rep_count, share),
        out_shape=(array(blocks, faces),) * vol_count,
        in_specs=[smem] + [vmem] * (1 + rep_count),
        out_specs=(vmem,) * vol_count,
        compiler_params=params,
    )(places, projection, *[move[d] for d in range(rep_count)]))
    moved = [swap(piece, "vol", d) if d else piece for d, piece in enumerate(moved)]

    info = pl.pallas_call(
        functools.partial(slope_kernel, rep_count, slab),
        out_shape=array(partner_count + 2, total, faces),
        in_specs=[vmem, pl.BlockSpec(memory_space=pl.ANY)],
        out_specs=vmem,
        scratch_shapes=[
            scratch(total, faces),
            scratch(6 * faces, partner_count * faces, dtype=jnp.bfloat16),
            scratch(partner_count, total, 2 * faces, dtype=jnp.bfloat16),
            scratch(partner_count, total, 2 * faces, dtype=jnp.bfloat16),
            scratch(LANES, LANES),
            pltpu.SemaphoreType.DMA,
        ],
        compiler_params=params,
    )(packed, mortar.reshape(partner_count * faces, faces))

    turns = list(range(vol_count))
    turns.insert(vol_count // 2 + 1, turns.pop(vol_count // 2 - 1))
    summed = pl.pallas_call(
        functools.partial(contact_kernel, tuple(order), tuple(turns)),
        out_shape=array(devices, slab, faces),
        in_specs=[smem] + [vmem] * (2 + vol_count),
        out_specs=vmem,
        scratch_shapes=[
            scratch(total, faces),
            scratch(total, faces),
            scratch(3 * faces, partner_count * faces, dtype=jnp.bfloat16),
            scratch(partner_count, 3 * faces, faces, dtype=jnp.bfloat16),
            scratch(partner_count, total, 2 * faces, dtype=jnp.bfloat16),
            scratch(partner_count, total, 2 * faces, dtype=jnp.bfloat16),
            scratch(total, faces),
            scratch(ROWS, total),
        ],
        compiler_params=params,
    )(places, stiffness, info, *[moved[d] for d in turns])
    summed, after = lax.optimization_barrier((summed, places))
    back_mix = pl.pallas_call(
        functools.partial(back_mixer_kernel, rep_count, share),
        out_shape=array(2, size, size, dtype=jnp.bfloat16),
        in_specs=[smem, vmem, smem],
        out_specs=vmem,
        compiler_params=params,
    )(places, projection, after)
    returned = lax.all_to_all(summed, ("vol", "rep"), 0, 0, tiled=True)

    pieces = pl.pallas_call(
        functools.partial(back_kernel, rep_count, share),
        out_shape=array(rep_count, slab * share, faces),
        in_specs=[vmem, vmem],
        out_specs=vmem,
        compiler_params=params,
    )(back_mix, returned)
    pieces = exchange([pieces[d] for d in range(rep_count)])
    out = jnp.zeros((blocks * share, faces), jnp.float32)
    for d in range(rep_count):
        out = lax.dynamic_update_slice_in_dim(out, pieces[d], (rep_index ^ d) * slab * share, 0)
    return out.reshape(blocks, share, faces)


def routed_local(surface_state, direction, stiffness, partners, contact_owner, projection, mortar):
    highest = lax.Precision.HIGHEST
    vol_count = lax.axis_size("vol")
    rep_index = lax.axis_index("rep")
    vol_index = lax.axis_index("vol")
    blocks, channel_share, face_count = surface_state.shape
    partner_count = partners.shape[1]
    capacity = max(2, (2 * blocks + vol_count - 1) // vol_count)
    slot_count = vol_count * capacity
    my_columns = lax.dynamic_slice_in_dim(projection, rep_index * channel_share, channel_share, 1)
    my_rows = lax.dynamic_slice_in_dim(projection, rep_index * channel_share, channel_share, 0)

    def fold_one(piece):
        return jnp.einsum("ij,bjf->bif", my_rows, piece, precision=highest)

    counter = jnp.arange(blocks, dtype=jnp.int32)
    same_owner = contact_owner[:, None] == contact_owner[None, :]
    earlier = counter[:, None] < counter[None, :]
    bucket_rank = jnp.sum((same_owner & earlier).astype(jnp.int32), axis=0)
    slot_of = contact_owner * capacity + bucket_rank
    slot_iota = jnp.arange(slot_count, dtype=jnp.int32)
    matches = slot_iota[:, None] == slot_of[None, :]
    occupied = jnp.any(matches, axis=1).astype(jnp.float32)
    source_row = jnp.sum(jnp.where(matches, counter[None, :], 0), axis=1)
    global_ids = vol_index * blocks + counter
    labels = jnp.concatenate([(global_ids + 1)[:, None], partners], axis=1).astype(jnp.float32)
    send_stiff = (stiffness[source_row] * occupied[:, None]).reshape(
        vol_count, capacity, face_count
    )
    send_labels = (labels[source_row] * occupied[:, None]).reshape(
        vol_count, capacity, partner_count + 1
    )

    def pack(values):
        return (values[source_row] * occupied[:, None, None]).reshape(
            vol_count, capacity, channel_share, face_count
        )

    projected = fold_one(lax.all_gather(surface_state, "rep", axis=1, tiled=True))
    moving = fold_one(lax.all_gather(direction, "rep", axis=1, tiled=True))
    received = (
        lax.all_to_all(pack(projected), "vol", split_axis=0, concat_axis=0, tiled=True),
        lax.all_to_all(pack(moving), "vol", split_axis=0, concat_axis=0, tiled=True),
        lax.all_to_all(send_stiff, "vol", split_axis=0, concat_axis=0, tiled=True),
        lax.all_to_all(send_labels, "vol", split_axis=0, concat_axis=0, tiled=True),
    )
    got_state = received[0].reshape(slot_count, channel_share, face_count)
    got_move = received[1].reshape(slot_count, channel_share, face_count)
    got_stiff = received[2].reshape(slot_count, face_count)
    got_labels = received[3].reshape(slot_count, partner_count + 1).astype(jnp.int32)
    slot_ids = got_labels[:, 0] - 1
    partner_ids = got_labels[:, 1:]
    partner_source = partner_ids // blocks
    candidates = slot_ids.reshape(vol_count, capacity)[partner_source]
    offsets = jnp.arange(capacity, dtype=jnp.int32)
    matched = candidates == partner_ids[..., None]
    found = jnp.any(matched, axis=2).astype(jnp.float32)
    partner_offset = jnp.sum(jnp.where(matched, offsets, 0), axis=2)
    partner_slot = partner_source * capacity + partner_offset
    mapped_state = jnp.einsum("rcf,kfg->krcg", got_state, mortar, precision=highest)
    weights = []
    for column in range(partner_count):
        target = partner_slot[:, column]
        contact_gap = got_state - mapped_state[column][target]
        squashed = jax.nn.sigmoid(sharpness * contact_gap)
        weights.append(
            found[:, column][:, None, None]
            * got_stiff[:, None, :]
            * sharpness
            * squashed
            * (1.0 - squashed)
        )
    partner_slot, weights = (partner_slot, weights)
    mapped_move = jnp.einsum("rcf,kfg->krcg", got_move, mortar, precision=highest)
    tangent = jnp.zeros_like(got_move)
    returns = []
    for column in range(partner_count):
        target = partner_slot[:, column]
        traction = weights[column] * (got_move - mapped_move[column][target])
        tangent = tangent + traction
        returns.append(jax.ops.segment_sum(traction, target, num_segments=slot_count))
    returned = jnp.einsum("krcg,kfg->rcf", jnp.stack(returns), mortar, precision=highest)
    summed = (tangent - returned).reshape(vol_count, capacity, channel_share, face_count)
    returned_tiles = lax.all_to_all(summed, "vol", split_axis=0, concat_axis=0, tiled=True)
    own_tangent = returned_tiles.reshape(slot_count, channel_share, face_count)[slot_of]
    return jnp.einsum(
        "ji,bjf->bif",
        my_columns,
        lax.all_gather(own_tangent, "rep", axis=1, tiled=True),
        precision=highest,
    )


def one_channel_each(mesh, state_shape, partner_shape):
    vol_count, rep_count = mesh.shape["vol"], mesh.shape["rep"]
    total, channels, faces = state_shape
    blocks = total // vol_count
    powers = all(n & (n - 1) == 0 for n in (vol_count, rep_count))
    return (
        powers
        and channels == vol_count * rep_count
        and channels // rep_count == ROWS
        and faces == LANES
        and blocks <= faces
        and blocks % (ROWS // 2 * rep_count) == 0
        and blocks % (2 * ROWS) == 0
        and ROWS % rep_count == 0
        and blocks // rep_count >= ROWS
        and min(vol_count, rep_count) > 1
        and total % LANES == 0
        and partner_shape[1] < ROWS
        and partner_shape[1] * LANES <= total
    )


def solution(mesh):
    placed = (
        P("vol", "rep", None),
        P("vol", "rep", None),
        P("vol", None),
        P("vol", None),
        P("vol"),
        P(),
        P(),
    )

    def program(surface_state, direction, stiffness, partners, *rest):
        fits = one_channel_each(mesh, surface_state.shape, partners.shape)
        plan = spread_local if fits else routed_local
        return jax.shard_map(
            plan, mesh=mesh, in_specs=placed, out_specs=P("vol", "rep", None), check_vma=False
        )(surface_state, direction, stiffness, partners, *rest)

    return program
```
